1024 devices in a mesh: row: 16 (over x, core), col: 16 (over y, z_lo), depth: 4 (over z_hi).
Axes of the slice: x: 8, y: 8, z: 8 (z_hi: 4, z_lo: 2; z = z_hi * 2 + z_lo), core: 2. Of those that a mesh axis runs over, the one named last changes fastest.
Arguments:
- density: bfloat16 [8192, 8192], P('row', 'col'), may hold values from -1.5 to 1.5
- pattern: int32 [128, 16], P('row'), may hold values from 0 to 127, all different within a row
- orbital_counts: int32 [16, 128], P('row'), may hold values from 1 to 9, 512 in all within a row
- branch_flag: int32 [128], P('row'), may hold values from 0 to 1
Outputs:
- updated: bfloat16 [8192, 8192], P('row', ('col', 'depth'))
- populations: float32 [2048], P('row')
The draws below stay inside these ranges and needn't reach their ends.
Inputs may be any that keep to these rules, and one draw needn't show every extreme that they name: `pattern`: each row names distinct block columns. `orbital_counts`: each row sums to 512.
All inputs are finite; a program needn't handle non-finite values.
Results may differ from the reference program's by a relative error of at most 0.007.
Values may be sent and summed in bfloat16 or wider, within the bound.
No kernel may reach another device: no remote copies, remote signals or barrier semaphores. Data moves between devices by JAX's collectives and lax.ppermute only.
A program may use at most 32 MiB of HBM per device.

```python
import math
import jax
import jax.numpy as jnp
import numpy as np
from jax import lax

BLOCK = 64
PATTERN = 16
TILE = 512
NORB = 8192
NBLK = 128
ATOMS_DEV = 128
ATOMS = 2048
N_ROW = 16


def place_ends(entries, rng, smallest, largest):
    dims = entries.shape
    place = [jax.random.randint(jax.random.fold_in(rng, axis), (), 0, dims[axis]) for axis in range(len(dims))]
    entries = entries.at[tuple(place)].set(smallest)
    longest = dims.index(max(dims))
    place[longest] = (place[longest] + 1) % dims[longest]
    return entries.at[tuple(place)].set(largest)


def block_scale(rng, extent, shards, smallest, high):
    loudness = 1.0
    for position, shards_of in shards:
        draws = jax.random.uniform(jax.random.fold_in(jax.random.fold_in(rng, 6), position), (shards_of,), jnp.float32, smallest / len(shards), high / len(shards))
        loudness = loudness * jnp.repeat(jnp.exp(draws), extent[position] // shards_of).reshape((-1,) + (1,) * (len(extent) - 1 - position))
    return loudness


def distinct(rng, rows, amount, top, lift):
    sequence = jax.random.permutation(jax.random.fold_in(rng, 1), amount)
    favour = sequence
    for power in range(3):
        favour = favour * favour // amount
    favour = favour * lift // amount
    tickets = jax.random.randint(jax.random.fold_in(rng, 2), (rows, amount), 0, 4096) + favour
    fixed_rows = jax.random.permutation(jax.random.fold_in(rng, 3), rows)[jnp.arange(amount) % rows]
    tickets = jnp.where(jnp.arange(rows)[:, None] == fixed_rows[None, :], 1 << 14, tickets)
    score = tickets * amount + jnp.arange(amount)
    return lax.top_k(score.astype(jnp.int32), top)[1].astype(jnp.int32)


def split_up(count, total, limit, skew):
    loads = [(1 << 20) // math.isqrt(rank ** skew) + 1 for rank in range(2, count + 1)]
    spare, holding = total - limit - (count - 1), [1] * (count - 1)
    while spare > 0:
        free = [i for i in range(count - 1) if holding[i] < limit]
        whole, budget = sum([loads[i] for i in free]), spare
        for i in free:
            addition = min(limit - holding[i], max(1, budget * loads[i] // whole), spare)
            holding[i] = holding[i] + addition
            spare = spare - addition
    return np.array([limit] + holding)


def ragged(key, count, total, bound, lean):
    if count == 2:
        one = jax.random.randint(key, (), max(1, total - bound), min(bound, total - 1) + 1)
        return jnp.stack([one, total - one])
    sizes = jnp.asarray(split_up(count, total, bound, lean), jnp.int32)
    pairs = (count - 1) // 2
    source_of, taker = sizes[1:1 + 2 * pairs:2], sizes[2:2 + 2 * pairs:2]
    room = jnp.minimum(source_of - 1, bound - taker)
    passed = jax.random.randint(jax.random.fold_in(key, 1), (pairs,), 0, 1 << 20) % (room + 1)
    sizes = sizes.at[1:1 + 2 * pairs:2].set(source_of - passed).at[2:2 + 2 * pairs:2].set(taker + passed)
    return sizes[jax.random.permutation(jax.random.fold_in(key, 2), count)]


def bell_draw(own_key, dims, width, most, split=(), kind=jnp.bfloat16):
    gain = block_scale(own_key, dims, split, -0.22, 0.18) if split else 1.0
    entries = jax.random.normal(own_key, dims, jnp.float32) * width * gain
    return jnp.minimum(jnp.maximum(entries, -most), most).astype(kind)


def setup_inputs(seed: int = 0) -> dict:
    streams_of = jax.random.split(jax.random.key(seed), 5)
    return {
        "density": bell_draw(streams_of[0], (NORB, NORB), 0.25, 1.5, ((0, 16), (1, 16))),
        "pattern": distinct(streams_of[1], NBLK, NBLK, PATTERN, 1024),
        "orbital_counts": jax.vmap(lambda own: ragged(own, ATOMS_DEV, TILE, 9, 1))(jax.random.split(streams_of[2], N_ROW)).reshape((N_ROW, ATOMS_DEV)).astype(jnp.int32),
        "branch_flag": place_ends(jax.random.randint(streams_of[3], (NBLK,), 0, 2), jax.random.fold_in(streams_of[3], 1), 0, 1).astype(jnp.int32),
    }


def keep_mask(pattern):
    block_ids = jnp.arange(NBLK, dtype=jnp.int32)
    listed = jnp.any(pattern[:, :, None] == block_ids[None, None, :], axis=1)
    block_keep = listed | (block_ids[:, None] == block_ids[None, :])
    return jnp.repeat(jnp.repeat(block_keep, BLOCK, axis=0), BLOCK, axis=1)


def reference(density, pattern, orbital_counts, branch_flag):
    full_mask = keep_mask(pattern)
    masked = jnp.where(full_mask, density, jnp.zeros_like(density))
    squared = jnp.dot(masked, masked, preferred_element_type=jnp.float32)
    reflected = 2.0 * masked.astype(jnp.float32) - squared
    row_flags = jnp.repeat(branch_flag, BLOCK)
    chosen = jnp.where(row_flags[:, None] == 1, squared, reflected)
    updated = jnp.where(full_mask, chosen, jnp.zeros_like(chosen)).astype(jnp.bfloat16)
    diagonal_vals = jnp.diagonal(updated).astype(jnp.float32).reshape(N_ROW, TILE)
    atom_ends = jnp.cumsum(orbital_counts, axis=1).astype(jnp.int32)
    atom_starts = atom_ends - orbital_counts
    positions = jnp.arange(TILE, dtype=jnp.int32)
    membership = ((positions[None, None, :] >= atom_starts[:, :, None]) & (positions[None, None, :] < atom_ends[:, :, None])).astype(jnp.float32)
    populations = jnp.einsum("gat,gt->ga", membership, diagonal_vals, precision=lax.Precision.HIGHEST)
    return updated, populations.reshape(ATOMS)
```

```python
import functools

import jax
import jax.numpy as jnp
from jax import lax
from jax.experimental import pallas as pl
from jax.experimental.pallas import tpu as pltpu
from jax.sharding import PartitionSpec as P

BLOCK = 64
VMEM = pl.BlockSpec(memory_space=pltpu.VMEM)
SMEM = pl.BlockSpec(memory_space=pltpu.SMEM)
F32 = jnp.float32
BF16 = jnp.bfloat16


def lanes(rows, count):
    return lax.broadcasted_iota(jnp.int32, (rows, count), 1)


def block_bits(pat_ref, block_row, own_block, first_col, count):
    bits = jnp.int32(0)
    for slot in range(pat_ref.shape[1] + 1):
        listed = own_block if slot == pat_ref.shape[1] else pat_ref[block_row, slot]
        local = listed - first_col
        inside = (local >= 0) & (local < count)
        bits = bits | jnp.where(inside, jnp.int32(1) << jnp.clip(local, 0, count - 1), 0)
    return bits


def pack_kernel(ids_ref, pat_ref, dens_ref, strip_ref, rows_ref, slots_ref, blocks):
    row, col, depth = ids_ref[0], ids_ref[1], ids_ref[2]
    n_rows, names = pat_ref.shape
    tile = dens_ref.shape[1]
    n_cols = tile // BLOCK
    width = strip_ref.shape[1]
    part = rows_ref.shape[0]
    first_col = col * n_cols
    start = pl.multiple_of(depth * width, width)
    which = lanes(BLOCK, width) // BLOCK
    for i in range(n_rows):
        bits = block_bits(pat_ref, i, row * n_rows + i, first_col, n_cols)
        keep = (lax.shift_right_logical(bits, depth * (width // BLOCK)) >> which) & 1
        here = pl.ds(i * BLOCK, BLOCK)
        value = dens_ref[here, pl.ds(start, width)].astype(F32)
        strip_ref[here, :] = jnp.where(keep == 1, value, 0.0).astype(BF16)
    first_row = depth * (part // BLOCK)
    begin = pl.multiple_of(depth * part, part)
    which = lanes(BLOCK, tile) // BLOCK
    blocks[n_cols] = jnp.zeros_like(blocks[n_cols])
    for u in range(part // BLOCK):
        i = first_row + u
        bits = block_bits(pat_ref, i, row * n_rows + i, first_col, n_cols)
        value = dens_ref[pl.ds(pl.multiple_of(begin + u * BLOCK, BLOCK), BLOCK), :].astype(F32)
        value = jnp.where(((bits >> which) & 1) == 1, value, 0.0)
        here = pl.ds(u * BLOCK, BLOCK)
        rows_ref[here, :] = value.astype(BF16)
        for j in range(n_cols):
            one = value[:, j * BLOCK : (j + 1) * BLOCK]
            blocks[j, here, :] = jnp.concatenate([one, one], axis=1)
    left = lanes(BLOCK, 2 * BLOCK) < BLOCK
    for u in range(part // BLOCK):
        i = first_row + u
        own_block = row * n_rows + i
        here = pl.ds(u * BLOCK, BLOCK)
        places = []
        repeated = jnp.int32(0)
        for slot in range(names):
            listed = pat_ref[i, slot]
            local = listed - first_col
            places.append(jnp.where((local >= 0) & (local < n_cols), local, n_cols))
            repeated = repeated | jnp.where(listed == own_block, 1, 0)
        local = own_block - first_col
        inside = (local >= 0) & (local < n_cols) & (repeated == 0)
        places.append(jnp.where(inside, local, n_cols))
        places.append(jnp.int32(n_cols))
        for pair in range(len(places) // 2):
            value = jnp.where(
                left, blocks[places[2 * pair], here, :], blocks[places[2 * pair + 1], here, :]
            )
            slots_ref[here, pair * 2 * BLOCK : (pair + 1) * 2 * BLOCK] = value.astype(BF16)


def share_kernel(ids_ref, flag_ref, rows_ref, trans_ref, parts_ref, out_ref):
    row, col, depth = ids_ref[0], ids_ref[1], ids_ref[2]
    part, tile = rows_ref.shape
    total = parts_ref[0].astype(F32)
    for source in range(1, parts_ref.shape[0]):
        total = total + parts_ref[source].astype(F32)
    product = jnp.dot(rows_ref[...], trans_ref[...], preferred_element_type=F32)
    eye = lax.broadcasted_iota(jnp.int32, (part, part), 0) == lanes(part, part)
    share = jnp.sum(jnp.where(eye, product, 0.0), axis=0, keepdims=True)
    on_diag = lax.broadcasted_iota(jnp.int32, (part, part), 0) == lanes(part, part)
    own = rows_ref[:, pl.ds(pl.multiple_of(depth * part, part), part)].astype(F32)
    own = jnp.sum(jnp.where(on_diag, own, 0.0), axis=0, keepdims=True)
    twice = jnp.where(row == col, 2.0, 0.0) * own
    first = depth * (part // BLOCK)
    flags = jnp.where(lanes(1, part) < BLOCK, flag_ref[first], flag_ref[first + 1])
    share = jnp.where(flags == 1, share, twice - share)
    rows8 = lax.broadcasted_iota(jnp.int32, (8, part), 0)
    full = jnp.broadcast_to(share, (8, part))
    base = jnp.where(rows8 % 2 == 0, pltpu.roll(full, BLOCK, 1), full)
    high = base.astype(BF16).astype(F32)
    middle = (base - high).astype(BF16).astype(F32)
    low = (base - high - middle).astype(BF16).astype(F32)
    terms = jnp.where(rows8 < 2, high, jnp.where(rows8 < 4, middle, jnp.where(rows8 < 6, low, 0.0)))
    wide = total.shape[1]
    last = jnp.where(lanes(8, part) < BLOCK, total[:, wide - part :], terms)
    send = jnp.concatenate([total[:, : wide - part], last], axis=1).astype(BF16)
    for target in range(out_ref.shape[0]):
        out_ref[target] = send


def product_kernel(
    ids_ref, pat_ref, flag_ref, count_ref, strip_ref, slots_ref, full_ref, out_ref, pop_ref, chosen
):
    row, col, depth = ids_ref[0], ids_ref[1], ids_ref[2]
    n_rows, names = pat_ref.shape
    width = strip_ref.shape[1]
    first_col = col * n_rows
    which = lanes(BLOCK, width) // BLOCK
    used = (names + 1) * BLOCK
    for i in range(n_rows):
        bits = block_bits(pat_ref, i, row * n_rows + i, first_col, n_rows)
        keep = (lax.shift_right_logical(bits, depth * (width // BLOCK)) >> which) & 1
        chosen[i, used:, :] = jnp.zeros_like(chosen[i, used:, :])
        for slot in range(names + 1):
            listed = row * n_rows + i if slot == names else pat_ref[i, slot]
            source = pl.ds(pl.multiple_of(listed * BLOCK, BLOCK), BLOCK)
            chosen[i, slot * BLOCK : (slot + 1) * BLOCK, :] = full_ref[source, :]
        here = pl.ds(i * BLOCK, BLOCK)
        squared = jnp.dot(slots_ref[here, :], chosen[i], preferred_element_type=F32)
        own = strip_ref[here, :].astype(F32)
        flag = jnp.broadcast_to(flag_ref[i], squared.shape)
        value = jnp.where(flag == 1, squared, 2.0 * own - squared)
        out_ref[here, :] = jnp.where(keep == 1, value, 0.0).astype(BF16)
    atoms = count_ref.shape[1]
    span = 2 * BLOCK
    wide = slots_ref.shape[1]
    low = lax.broadcasted_iota(jnp.int32, (atoms, atoms), 0)
    counts = jnp.broadcast_to(count_ref[...].astype(F32), (atoms, atoms))
    ends = jnp.sum(jnp.where(lanes(atoms, atoms) <= low, counts, 0.0), axis=1, keepdims=True)
    starts = jnp.sum(jnp.where(lanes(atoms, atoms) < low, counts, 0.0), axis=1, keepdims=True)
    at = lanes(atoms, span)
    total = jnp.zeros((atoms, span), F32)
    per_depth = 2 * BLOCK
    for d in range(n_rows // 2):
        terms = slots_ref[d * per_depth : (d + 1) * per_depth, wide - span :].astype(F32)
        terms = jnp.sum(terms.reshape(per_depth // 8, 8, span), axis=0)
        diag = terms[0:2] + terms[2:4] + terms[4:6]
        diag = diag.astype(BF16).astype(F32)
        for u in range(2):
            place = (at + ((2 * d + u) * BLOCK - BLOCK)).astype(F32)
            inside = (place >= starts) & (place < ends) & (at >= BLOCK)
            total = total + jnp.where(inside, jnp.broadcast_to(diag[u : u + 1], (atoms, span)), 0.0)
    ones = jnp.ones((8, span), F32)
    sums = lax.dot_general(
        ones, total, (((1,), (1,)), ((), ())), precision=lax.Precision.HIGHEST, preferred_element_type=F32
    )
    pop_ref[...] = sums[0:1]


def per_device(density, pattern, orbital_counts, branch_flag):
    tile = density.shape[0]
    n_row, n_col, n_depth = (lax.axis_size(name) for name in ("row", "col", "depth"))
    width = tile // n_depth
    n_rows, names = pattern.shape
    slots_wide = (names + 2) * BLOCK
    ids = jnp.stack([lax.axis_index("row"), lax.axis_index("col"), lax.axis_index("depth")]).astype(jnp.int32)
    limit = pltpu.CompilerParams(vmem_limit_bytes=48 << 20)
    strip, rows, slots = pl.pallas_call(
        pack_kernel,
        out_shape=(
            jax.ShapeDtypeStruct((tile, width), BF16),
            jax.ShapeDtypeStruct((width, tile), BF16),
            jax.ShapeDtypeStruct((width, slots_wide), BF16),
        ),
        in_specs=[SMEM, SMEM, VMEM],
        out_specs=(VMEM, VMEM, VMEM),
        scratch_shapes=[pltpu.VMEM((tile // BLOCK + 1, width, 2 * BLOCK), F32)],
        compiler_params=limit,
        name="pack",
    )(ids, pattern, density)
    full = lax.all_gather(strip, "row", axis=0, tiled=True)
    swap = [(r * n_col + c, c * n_col + r) for r in range(n_row) for c in range(n_col)]
    trans = lax.ppermute(strip, ("row", "col"), swap)
    chunk = width // n_col
    parts = lax.all_to_all(slots.reshape(n_col, chunk, slots_wide), "col", 0, 0)
    send = pl.pallas_call(
        share_kernel,
        out_shape=jax.ShapeDtypeStruct((n_depth * n_col, chunk, slots_wide), BF16),
        in_specs=[SMEM, SMEM, VMEM, VMEM, VMEM],
        out_specs=VMEM,
        compiler_params=limit,
        name="share",
    )(ids, branch_flag, rows, trans, parts)
    stripe = lax.all_to_all(send, ("depth", "col"), 0, 0).reshape(tile, slots_wide)
    updated, populations = pl.pallas_call(
        product_kernel,
        out_shape=(
            jax.ShapeDtypeStruct((tile, width), BF16),
            jax.ShapeDtypeStruct((1, orbital_counts.shape[1]), F32),
        ),
        in_specs=[SMEM, SMEM, SMEM, VMEM, VMEM, VMEM, VMEM],
        out_specs=(VMEM, VMEM),
        scratch_shapes=[pltpu.VMEM((n_rows, slots_wide, width), BF16)],
        compiler_params=limit,
        name="product",
    )(ids, pattern, branch_flag, orbital_counts, strip, stripe, full)
    return (updated, populations.reshape(-1))


def solution(mesh):
    in_specs = (P("row", "col"), P("row", None), P("row", None), P("row"))
    out_specs = (P("row", ("col", "depth")), P("row"))
    return jax.shard_map(
        per_device, mesh=mesh, in_specs=in_specs, out_specs=out_specs, check_vma=False
    )
```

```python
import functools

import jax
import jax.numpy as jnp
from jax import lax
from jax.experimental import pallas as pl
from jax.experimental.pallas import tpu as pltpu
from jax.sharding import PartitionSpec as P

BLOCK = 64
VMEM = pl.BlockSpec(memory_space=pltpu.VMEM)
SMEM = pl.BlockSpec(memory_space=pltpu.SMEM)
F32 = jnp.float32
BF16 = jnp.bfloat16


def lanes(rows, count):
    return lax.broadcasted_iota(jnp.int32, (rows, count), 1)


def block_bits(pat_ref, block_row, own_block, first_col, count):
    bits = jnp.int32(0)
    for slot in range(pat_ref.shape[1] + 1):
        listed = own_block if slot == pat_ref.shape[1] else pat_ref[block_row, slot]
        local = listed - first_col
        inside = (local >= 0) & (local < count)
        bits = bits | jnp.where(inside, jnp.int32(1) << jnp.clip(local, 0, count - 1), 0)
    return bits


def strip_kernel(ids_ref, pat_ref, dens_ref, strip_ref):
    row, col, depth = ids_ref[0], ids_ref[1], ids_ref[2]
    n_rows = pat_ref.shape[0]
    width = strip_ref.shape[1]
    first_col = col * n_rows
    start = pl.multiple_of(depth * width, width)
    which = lanes(BLOCK, width) // BLOCK
    for i in range(n_rows):
        bits = block_bits(pat_ref, i, row * n_rows + i, first_col, n_rows)
        keep = (lax.shift_right_logical(bits, depth * (width // BLOCK)) >> which) & 1
        here = pl.ds(i * BLOCK, BLOCK)
        value = dens_ref[here, pl.ds(start, width)].astype(F32)
        strip_ref[here, :] = jnp.where(keep == 1, value, 0.0).astype(BF16)


def pack_kernel(ids_ref, pat_ref, dens_ref, rows_ref, slots_ref, blocks):
    row, col, depth = ids_ref[0], ids_ref[1], ids_ref[2]
    n_rows, names = pat_ref.shape
    tile = dens_ref.shape[1]
    n_cols = tile // BLOCK
    part = rows_ref.shape[0]
    first_col = col * n_cols
    first_row = depth * (part // BLOCK)
    begin = pl.multiple_of(depth * part, part)
    which = lanes(BLOCK, tile) // BLOCK
    blocks[n_cols] = jnp.zeros_like(blocks[n_cols])
    for u in range(part // BLOCK):
        i = first_row + u
        bits = block_bits(pat_ref, i, row * n_rows + i, first_col, n_cols)
        value = dens_ref[pl.ds(pl.multiple_of(begin + u * BLOCK, BLOCK), BLOCK), :].astype(F32)
        value = jnp.where(((bits >> which) & 1) == 1, value, 0.0)
        here = pl.ds(u * BLOCK, BLOCK)
        rows_ref[here, :] = value.astype(BF16)
        for j in range(n_cols):
            one = value[:, j * BLOCK : (j + 1) * BLOCK]
            blocks[j, here, :] = jnp.concatenate([one, one], axis=1)
    left = lanes(BLOCK, 2 * BLOCK) < BLOCK
    for u in range(part // BLOCK):
        i = first_row + u
        own_block = row * n_rows + i
        here = pl.ds(u * BLOCK, BLOCK)
        places = []
        repeated = jnp.int32(0)
        for slot in range(names):
            listed = pat_ref[i, slot]
            local = listed - first_col
            places.append(jnp.where((local >= 0) & (local < n_cols), local, n_cols))
            repeated = repeated | jnp.where(listed == own_block, 1, 0)
        local = own_block - first_col
        inside = (local >= 0) & (local < n_cols) & (repeated == 0)
        places.append(jnp.where(inside, local, n_cols))
        places.append(jnp.int32(n_cols))
        for pair in range(len(places) // 2):
            value = jnp.where(
                left, blocks[places[2 * pair], here, :], blocks[places[2 * pair + 1], here, :]
            )
            slots_ref[here, pair * 2 * BLOCK : (pair + 1) * 2 * BLOCK] = value.astype(BF16)


def share_kernel(ids_ref, flag_ref, rows_ref, trans_ref, parts_ref, out_ref):
    row, col, depth = ids_ref[0], ids_ref[1], ids_ref[2]
    part, tile = rows_ref.shape
    total = parts_ref[0].astype(F32)
    for source in range(1, parts_ref.shape[0]):
        total = total + parts_ref[source].astype(F32)
    product = jnp.dot(rows_ref[...], trans_ref[...], preferred_element_type=F32)
    eye = lax.broadcasted_iota(jnp.int32, (part, part), 0) == lanes(part, part)
    share = jnp.sum(jnp.where(eye, product, 0.0), axis=0, keepdims=True)
    on_diag = lax.broadcasted_iota(jnp.int32, (part, part), 0) == lanes(part, part)
    own = rows_ref[:, pl.ds(pl.multiple_of(depth * part, part), part)].astype(F32)
    own = jnp.sum(jnp.where(on_diag, own, 0.0), axis=0, keepdims=True)
    twice = jnp.where(row == col, 2.0, 0.0) * own
    first = depth * (part // BLOCK)
    flags = jnp.where(lanes(1, part) < BLOCK, flag_ref[first], flag_ref[first + 1])
    share = jnp.where(flags == 1, share, twice - share)
    rows8 = lax.broadcasted_iota(jnp.int32, (8, part), 0)
    full = jnp.broadcast_to(share, (8, part))
    base = jnp.where(rows8 % 2 == 0, pltpu.roll(full, BLOCK, 1), full)
    high = base.astype(BF16).astype(F32)
    middle = (base - high).astype(BF16).astype(F32)
    low = (base - high - middle).astype(BF16).astype(F32)
    terms = jnp.where(rows8 < 2, high, jnp.where(rows8 < 4, middle, jnp.where(rows8 < 6, low, 0.0)))
    wide = total.shape[1]
    last = jnp.where(lanes(8, part) < BLOCK, total[:, wide - part :], terms)
    send = jnp.concatenate([total[:, : wide - part], last], axis=1).astype(BF16)
    for target in range(out_ref.shape[0]):
        out_ref[target] = send


def product_kernel(
    ids_ref, pat_ref, flag_ref, count_ref, strip_ref, slots_ref, full_ref, out_ref, pop_ref, chosen
):
    row, col, depth = ids_ref[0], ids_ref[1], ids_ref[2]
    n_rows, names = pat_ref.shape
    width = strip_ref.shape[1]
    first_col = col * n_rows
    which = lanes(BLOCK, width) // BLOCK
    used = (names + 1) * BLOCK
    for i in range(n_rows):
        bits = block_bits(pat_ref, i, row * n_rows + i, first_col, n_rows)
        keep = (lax.shift_right_logical(bits, depth * (width // BLOCK)) >> which) & 1
        chosen[i, used:, :] = jnp.zeros_like(chosen[i, used:, :])
        for slot in range(names + 1):
            listed = row * n_rows + i if slot == names else pat_ref[i, slot]
            source = pl.ds(pl.multiple_of(listed * BLOCK, BLOCK), BLOCK)
            chosen[i, slot * BLOCK : (slot + 1) * BLOCK, :] = full_ref[source, :]
        here = pl.ds(i * BLOCK, BLOCK)
        squared = jnp.dot(slots_ref[here, :], chosen[i], preferred_element_type=F32)
        own = strip_ref[here, :].astype(F32)
        flag = jnp.broadcast_to(flag_ref[i], squared.shape)
        value = jnp.where(flag == 1, squared, 2.0 * own - squared)
        out_ref[here, :] = jnp.where(keep == 1, value, 0.0).astype(BF16)
    atoms = count_ref.shape[1]
    span = 2 * BLOCK
    wide = slots_ref.shape[1]
    low = lax.broadcasted_iota(jnp.int32, (atoms, atoms), 0)
    counts = jnp.broadcast_to(count_ref[...].astype(F32), (atoms, atoms))
    ends = jnp.sum(jnp.where(lanes(atoms, atoms) <= low, counts, 0.0), axis=1, keepdims=True)
    starts = jnp.sum(jnp.where(lanes(atoms, atoms) < low, counts, 0.0), axis=1, keepdims=True)
    at = lanes(atoms, span)
    total = jnp.zeros((atoms, span), F32)
    per_depth = 2 * BLOCK
    for d in range(n_rows // 2):
        terms = slots_ref[d * per_depth : (d + 1) * per_depth, wide - span :].astype(F32)
        terms = jnp.sum(terms.reshape(per_depth // 8, 8, span), axis=0)
        diag = terms[0:2] + terms[2:4] + terms[4:6]
        diag = diag.astype(BF16).astype(F32)
        for u in range(2):
            place = (at + ((2 * d + u) * BLOCK - BLOCK)).astype(F32)
            inside = (place >= starts) & (place < ends) & (at >= BLOCK)
            total = total + jnp.where(inside, jnp.broadcast_to(diag[u : u + 1], (atoms, span)), 0.0)
    ones = jnp.ones((8, span), F32)
    sums = lax.dot_general(
        ones, total, (((1,), (1,)), ((), ())), precision=lax.Precision.HIGHEST, preferred_element_type=F32
    )
    pop_ref[...] = sums[0:1]


def per_device(density, pattern, orbital_counts, branch_flag):
    tile = density.shape[0]
    n_row, n_col, n_depth = (lax.axis_size(name) for name in ("row", "col", "depth"))
    width = tile // n_depth
    n_rows, names = pattern.shape
    slots_wide = (names + 2) * BLOCK
    ids = jnp.stack([lax.axis_index("row"), lax.axis_index("col"), lax.axis_index("depth")]).astype(jnp.int32)
    limit = pltpu.CompilerParams(vmem_limit_bytes=48 << 20)
    strip = pl.pallas_call(
        strip_kernel,
        out_shape=jax.ShapeDtypeStruct((tile, width), BF16),
        in_specs=[SMEM, SMEM, VMEM],
        out_specs=VMEM,
        compiler_params=limit,
        name="strip",
    )(ids, pattern, density)
    full = lax.all_gather(strip, "row", axis=0, tiled=True)
    swap = [(r * n_col + c, c * n_col + r) for r in range(n_row) for c in range(n_col)]
    trans = lax.ppermute(strip, ("row", "col"), swap)
    rows, slots = pl.pallas_call(
        pack_kernel,
        out_shape=(
            jax.ShapeDtypeStruct((width, tile), BF16),
            jax.ShapeDtypeStruct((width, slots_wide), BF16),
        ),
        in_specs=[SMEM, SMEM, VMEM],
        out_specs=(VMEM, VMEM),
        scratch_shapes=[pltpu.VMEM((tile // BLOCK + 1, width, 2 * BLOCK), F32)],
        compiler_params=limit,
        name="pack",
    )(ids, pattern, density)
    chunk = width // n_col
    parts = lax.all_to_all(slots.reshape(n_col, chunk, slots_wide), "col", 0, 0)
    send = pl.pallas_call(
        share_kernel,
        out_shape=jax.ShapeDtypeStruct((n_depth * n_col, chunk, slots_wide), BF16),
        in_specs=[SMEM, SMEM, VMEM, VMEM, VMEM],
        out_specs=VMEM,
        compiler_params=limit,
        name="share",
    )(ids, branch_flag, rows, trans, parts)
    stripe = lax.all_to_all(send, ("depth", "col"), 0, 0).reshape(tile, slots_wide)
    updated, populations = pl.pallas_call(
        product_kernel,
        out_shape=(
            jax.ShapeDtypeStruct((tile, width), BF16),
            jax.ShapeDtypeStruct((1, orbital_counts.shape[1]), F32),
        ),
        in_specs=[SMEM, SMEM, SMEM, VMEM, VMEM, VMEM, VMEM],
        out_specs=(VMEM, VMEM),
        scratch_shapes=[pltpu.VMEM((n_rows, slots_wide, width), BF16)],
        compiler_params=limit,
        name="product",
    )(ids, pattern, branch_flag, orbital_counts, strip, stripe, full)
    return (updated, populations.reshape(-1))


def solution(mesh):
    in_specs = (P("row", "col"), P("row", None), P("row", None), P("row"))
    out_specs = (P("row", ("col", "depth")), P("row"))
    return jax.shard_map(
        per_device, mesh=mesh, in_specs=in_specs, out_specs=out_specs, check_vma=False
    )
```

```python
import functools

import jax
import jax.numpy as jnp
from jax import lax
from jax.experimental import pallas as pl
from jax.experimental.pallas import tpu as pltpu
from jax.sharding import PartitionSpec as P

BLOCK = 64
VMEM = pl.BlockSpec(memory_space=pltpu.VMEM)
SMEM = pl.BlockSpec(memory_space=pltpu.SMEM)
F32 = jnp.float32
BF16 = jnp.bfloat16
ORDER = (3, 2, 1, 0)


def lanes(rows, count):
    return lax.broadcasted_iota(jnp.int32, (rows, count), 1)


def block_bits(pat_ref, block_row, own_block, first_col, count):
    bits = jnp.int32(0)
    for slot in range(pat_ref.shape[1] + 1):
        listed = own_block if slot == pat_ref.shape[1] else pat_ref[block_row, slot]
        local = listed - first_col
        inside = (local >= 0) & (local < count)
        bits = bits | jnp.where(inside, jnp.int32(1) << jnp.clip(local, 0, count - 1), 0)
    return bits


def pack_kernel(ids_ref, pat_ref, dens_ref, strip_ref, rows_ref, slots_ref, blocks):
    row, col, depth = ids_ref[0], ids_ref[1], ids_ref[2]
    n_rows, names = pat_ref.shape
    tile = dens_ref.shape[1]
    n_cols = tile // BLOCK
    width = strip_ref.shape[1]
    part = rows_ref.shape[0]
    first_col = col * n_cols
    start = pl.multiple_of(depth * width, width)
    which = lanes(BLOCK, width) // BLOCK
    for i in range(n_rows):
        bits = block_bits(pat_ref, i, row * n_rows + i, first_col, n_cols)
        keep = (lax.shift_right_logical(bits, depth * (width // BLOCK)) >> which) & 1
        here = pl.ds(i * BLOCK, BLOCK)
        value = dens_ref[here, pl.ds(start, width)].astype(F32)
        strip_ref[here, :] = jnp.where(keep == 1, value, 0.0).astype(BF16)
    first_row = depth * (part // BLOCK)
    begin = pl.multiple_of(depth * part, part)
    which = lanes(BLOCK, tile) // BLOCK
    blocks[n_cols] = jnp.zeros_like(blocks[n_cols])
    for u in range(part // BLOCK):
        i = first_row + u
        bits = block_bits(pat_ref, i, row * n_rows + i, first_col, n_cols)
        value = dens_ref[pl.ds(pl.multiple_of(begin + u * BLOCK, BLOCK), BLOCK), :].astype(F32)
        value = jnp.where(((bits >> which) & 1) == 1, value, 0.0)
        here = pl.ds(u * BLOCK, BLOCK)
        rows_ref[here, :] = value.astype(BF16)
        for j in range(n_cols):
            one = value[:, j * BLOCK : (j + 1) * BLOCK]
            blocks[j, here, :] = jnp.concatenate([one, one], axis=1)
    left = lanes(BLOCK, 2 * BLOCK) < BLOCK
    for u in range(part // BLOCK):
        i = first_row + u
        own_block = row * n_rows + i
        here = pl.ds(u * BLOCK, BLOCK)
        places = []
        repeated = jnp.int32(0)
        for slot in range(names):
            listed = pat_ref[i, slot]
            local = listed - first_col
            places.append(jnp.where((local >= 0) & (local < n_cols), local, n_cols))
            repeated = repeated | jnp.where(listed == own_block, 1, 0)
        local = own_block - first_col
        inside = (local >= 0) & (local < n_cols) & (repeated == 0)
        places.append(jnp.where(inside, local, n_cols))
        places.append(jnp.int32(n_cols))
        for pair in range(len(places) // 2):
            value = jnp.where(
                left, blocks[places[2 * pair], here, :], blocks[places[2 * pair + 1], here, :]
            )
            slots_ref[here, pair * 2 * BLOCK : (pair + 1) * 2 * BLOCK] = value.astype(BF16)


def share_kernel(ids_ref, flag_ref, rows_ref, trans_ref, parts_ref, out_ref):
    row, col, depth = ids_ref[0], ids_ref[1], ids_ref[2]
    part, tile = rows_ref.shape
    total = parts_ref[0].astype(F32)
    for source in range(1, parts_ref.shape[0]):
        total = total + parts_ref[source].astype(F32)
    product = jnp.dot(rows_ref[...], trans_ref[...], preferred_element_type=F32)
    eye = lax.broadcasted_iota(jnp.int32, (part, part), 0) == lanes(part, part)
    share = jnp.sum(jnp.where(eye, product, 0.0), axis=0, keepdims=True)
    on_diag = lax.broadcasted_iota(jnp.int32, (part, part), 0) == lanes(part, part)
    own = rows_ref[:, pl.ds(pl.multiple_of(depth * part, part), part)].astype(F32)
    own = jnp.sum(jnp.where(on_diag, own, 0.0), axis=0, keepdims=True)
    twice = jnp.where(row == col, 2.0, 0.0) * own
    first = depth * (part // BLOCK)
    flags = jnp.where(lanes(1, part) < BLOCK, flag_ref[first], flag_ref[first + 1])
    share = jnp.where(flags == 1, share, twice - share)
    rows8 = lax.broadcasted_iota(jnp.int32, (8, part), 0)
    full = jnp.broadcast_to(share, (8, part))
    base = jnp.where(rows8 % 2 == 0, pltpu.roll(full, BLOCK, 1), full)
    high = base.astype(BF16).astype(F32)
    middle = (base - high).astype(BF16).astype(F32)
    low = (base - high - middle).astype(BF16).astype(F32)
    terms = jnp.where(rows8 < 2, high, jnp.where(rows8 < 4, middle, jnp.where(rows8 < 6, low, 0.0)))
    wide = total.shape[1]
    last = jnp.where(lanes(8, part) < BLOCK, total[:, wide - part :], terms)
    send = jnp.concatenate([total[:, : wide - part], last], axis=1).astype(BF16)
    for target in range(out_ref.shape[0]):
        out_ref[target] = send


def held_at(block_row, row, n_rows):
    differs = (block_row // n_rows) ^ row
    place = jnp.int32(0)
    for bit, axis_bit in enumerate(ORDER):
        place = place | (((differs >> axis_bit) & 1) << bit)
    return place * n_rows + block_row % n_rows


def gather_strip(strip):
    held = strip
    n_row = lax.axis_size("row")
    for axis_bit in ORDER:
        pairs = [(r, r ^ (1 << axis_bit)) for r in range(n_row)]
        other = lax.ppermute(held, "row", pairs)
        if axis_bit == ORDER[-1]:
            return held, other
        held = jnp.concatenate([held, other], axis=0)


def product_kernel(
    ids_ref, pat_ref, flag_ref, count_ref, strip_ref, slots_ref, even_ref, odd_ref, out_ref, pop_ref, full, chosen
):
    row, col, depth = ids_ref[0], ids_ref[1], ids_ref[2]
    n_rows, names = pat_ref.shape
    width = strip_ref.shape[1]
    first_col = col * n_rows
    which = lanes(BLOCK, width) // BLOCK
    used = (names + 1) * BLOCK
    half = even_ref.shape[0]
    full[0:half, :] = even_ref[...]
    full[half : 2 * half, :] = odd_ref[...]
    for i in range(n_rows):
        bits = block_bits(pat_ref, i, row * n_rows + i, first_col, n_rows)
        keep = (lax.shift_right_logical(bits, depth * (width // BLOCK)) >> which) & 1
        chosen[i, used:, :] = jnp.zeros_like(chosen[i, used:, :])
        for slot in range(names + 1):
            listed = row * n_rows + i if slot == names else pat_ref[i, slot]
            source = pl.ds(pl.multiple_of(held_at(listed, row, n_rows) * BLOCK, BLOCK), BLOCK)
            chosen[i, slot * BLOCK : (slot + 1) * BLOCK, :] = full[source, :]
        here = pl.ds(i * BLOCK, BLOCK)
        squared = jnp.dot(slots_ref[here, :], chosen[i], preferred_element_type=F32)
        own = strip_ref[here, :].astype(F32)
        flag = jnp.broadcast_to(flag_ref[i], squared.shape)
        value = jnp.where(flag == 1, squared, 2.0 * own - squared)
        out_ref[here, :] = jnp.where(keep == 1, value, 0.0).astype(BF16)
    atoms = count_ref.shape[1]
    span = 2 * BLOCK
    wide = slots_ref.shape[1]
    low = lax.broadcasted_iota(jnp.int32, (atoms, atoms), 0)
    counts = jnp.broadcast_to(count_ref[...].astype(F32), (atoms, atoms))
    ends = jnp.sum(jnp.where(lanes(atoms, atoms) <= low, counts, 0.0), axis=1, keepdims=True)
    starts = jnp.sum(jnp.where(lanes(atoms, atoms) < low, counts, 0.0), axis=1, keepdims=True)
    at = lanes(atoms, span)
    total = jnp.zeros((atoms, span), F32)
    per_depth = 2 * BLOCK
    for d in range(n_rows // 2):
        terms = slots_ref[d * per_depth : (d + 1) * per_depth, wide - span :].astype(F32)
        terms = jnp.sum(terms.reshape(per_depth // 8, 8, span), axis=0)
        diag = terms[0:2] + terms[2:4] + terms[4:6]
        diag = diag.astype(BF16).astype(F32)
        for u in range(2):
            place = (at + ((2 * d + u) * BLOCK - BLOCK)).astype(F32)
            inside = (place >= starts) & (place < ends) & (at >= BLOCK)
            total = total + jnp.where(inside, jnp.broadcast_to(diag[u : u + 1], (atoms, span)), 0.0)
    ones = jnp.ones((8, span), F32)
    sums = lax.dot_general(
        ones, total, (((1,), (1,)), ((), ())), precision=lax.Precision.HIGHEST, preferred_element_type=F32
    )
    pop_ref[...] = sums[0:1]


def per_device(density, pattern, orbital_counts, branch_flag):
    tile = density.shape[0]
    n_row, n_col, n_depth = (lax.axis_size(name) for name in ("row", "col", "depth"))
    width = tile // n_depth
    n_rows, names = pattern.shape
    slots_wide = (names + 2) * BLOCK
    ids = jnp.stack([lax.axis_index("row"), lax.axis_index("col"), lax.axis_index("depth")]).astype(jnp.int32)
    limit = pltpu.CompilerParams(vmem_limit_bytes=48 << 20)
    strip, rows, slots = pl.pallas_call(
        pack_kernel,
        out_shape=(
            jax.ShapeDtypeStruct((tile, width), BF16),
            jax.ShapeDtypeStruct((width, tile), BF16),
            jax.ShapeDtypeStruct((width, slots_wide), BF16),
        ),
        in_specs=[SMEM, SMEM, VMEM],
        out_specs=(VMEM, VMEM, VMEM),
        scratch_shapes=[pltpu.VMEM((tile // BLOCK + 1, width, 2 * BLOCK), F32)],
        compiler_params=limit,
        name="pack",
    )(ids, pattern, density)
    held, other = gather_strip(strip)
    swap = [(r * n_col + c, c * n_col + r) for r in range(n_row) for c in range(n_col)]
    trans = lax.ppermute(strip, ("row", "col"), swap)
    chunk = width // n_col
    parts = lax.all_to_all(slots.reshape(n_col, chunk, slots_wide), "col", 0, 0)
    send = pl.pallas_call(
        share_kernel,
        out_shape=jax.ShapeDtypeStruct((n_depth * n_col, chunk, slots_wide), BF16),
        in_specs=[SMEM, SMEM, VMEM, VMEM, VMEM],
        out_specs=VMEM,
        compiler_params=limit,
        name="share",
    )(ids, branch_flag, rows, trans, parts)
    stripe = lax.all_to_all(send, ("depth", "col"), 0, 0).reshape(tile, slots_wide)
    updated, populations = pl.pallas_call(
        product_kernel,
        out_shape=(
            jax.ShapeDtypeStruct((tile, width), BF16),
            jax.ShapeDtypeStruct((1, orbital_counts.shape[1]), F32),
        ),
        in_specs=[SMEM, SMEM, SMEM, VMEM, VMEM, VMEM, VMEM, VMEM],
        out_specs=(VMEM, VMEM),
        scratch_shapes=[
            pltpu.VMEM((n_row * tile, width), BF16),
            pltpu.VMEM((n_rows, slots_wide, width), BF16),
        ],
        compiler_params=limit,
        name="product",
    )(ids, pattern, branch_flag, orbital_counts, strip, stripe, held, other)
    return (updated, populations.reshape(-1))


def solution(mesh):
    in_specs = (P("row", "col"), P("row", None), P("row", None), P("row"))
    out_specs = (P("row", ("col", "depth")), P("row"))
    return jax.shard_map(
        per_device, mesh=mesh, in_specs=in_specs, out_specs=out_specs, check_vma=False
    )
```

```python
import functools

import jax
import jax.numpy as jnp
from jax import lax
from jax.experimental import pallas as pl
from jax.experimental.pallas import tpu as pltpu
from jax.sharding import PartitionSpec as P

BLOCK = 64
VMEM = pl.BlockSpec(memory_space=pltpu.VMEM)
SMEM = pl.BlockSpec(memory_space=pltpu.SMEM)
F32 = jnp.float32
BF16 = jnp.bfloat16
PLACES = 0x63517240


def lanes(rows, count):
    return lax.broadcasted_iota(jnp.int32, (rows, count), 1)


def block_bits(pat_ref, block_row, own_block, first_col, count):
    bits = jnp.int32(0)
    for slot in range(pat_ref.shape[1] + 1):
        listed = own_block if slot == pat_ref.shape[1] else pat_ref[block_row, slot]
        local = listed - first_col
        inside = (local >= 0) & (local < count)
        bits = bits | jnp.where(inside, jnp.int32(1) << jnp.clip(local, 0, count - 1), 0)
    return bits


def pack_kernel(ids_ref, pat_ref, dens_ref, strip_ref, rows_ref, slots_ref, blocks):
    row, col, depth = ids_ref[0], ids_ref[1], ids_ref[2]
    n_rows, names = pat_ref.shape
    tile = dens_ref.shape[1]
    n_cols = tile // BLOCK
    width = strip_ref.shape[1]
    part = rows_ref.shape[0]
    first_col = col * n_cols
    start = pl.multiple_of(depth * width, width)
    which = lanes(BLOCK, width) // BLOCK
    for i in range(n_rows):
        bits = block_bits(pat_ref, i, row * n_rows + i, first_col, n_cols)
        keep = (lax.shift_right_logical(bits, depth * (width // BLOCK)) >> which) & 1
        here = pl.ds(i * BLOCK, BLOCK)
        value = dens_ref[here, pl.ds(start, width)].astype(F32)
        strip_ref[here, :] = jnp.where(keep == 1, value, 0.0).astype(BF16)
    first_row = depth * (part // BLOCK)
    begin = pl.multiple_of(depth * part, part)
    which = lanes(BLOCK, tile) // BLOCK
    blocks[n_cols] = jnp.zeros_like(blocks[n_cols])
    for u in range(part // BLOCK):
        i = first_row + u
        bits = block_bits(pat_ref, i, row * n_rows + i, first_col, n_cols)
        value = dens_ref[pl.ds(pl.multiple_of(begin + u * BLOCK, BLOCK), BLOCK), :].astype(F32)
        value = jnp.where(((bits >> which) & 1) == 1, value, 0.0)
        here = pl.ds(u * BLOCK, BLOCK)
        rows_ref[here, :] = value.astype(BF16)
        for j in range(n_cols):
            one = value[:, j * BLOCK : (j + 1) * BLOCK]
            blocks[j, here, :] = jnp.concatenate([one, one], axis=1)
    left = lanes(BLOCK, 2 * BLOCK) < BLOCK
    for u in range(part // BLOCK):
        i = first_row + u
        own_block = row * n_rows + i
        here = pl.ds(u * BLOCK, BLOCK)
        places = []
        repeated = jnp.int32(0)
        for slot in range(names):
            listed = pat_ref[i, slot]
            local = listed - first_col
            places.append(jnp.where((local >= 0) & (local < n_cols), local, n_cols))
            repeated = repeated | jnp.where(listed == own_block, 1, 0)
        local = own_block - first_col
        inside = (local >= 0) & (local < n_cols) & (repeated == 0)
        places.append(jnp.where(inside, local, n_cols))
        places.append(jnp.int32(n_cols))
        for pair in range(len(places) // 2):
            value = jnp.where(
                left, blocks[places[2 * pair], here, :], blocks[places[2 * pair + 1], here, :]
            )
            slots_ref[here, pair * 2 * BLOCK : (pair + 1) * 2 * BLOCK] = value.astype(BF16)


def share_kernel(ids_ref, flag_ref, rows_ref, trans_ref, parts_ref, out_ref):
    row, col, depth = ids_ref[0], ids_ref[1], ids_ref[2]
    part, tile = rows_ref.shape
    total = parts_ref[0].astype(F32)
    for source in range(1, parts_ref.shape[0]):
        total = total + parts_ref[source].astype(F32)
    product = jnp.dot(rows_ref[...], trans_ref[...], preferred_element_type=F32)
    eye = lax.broadcasted_iota(jnp.int32, (part, part), 0) == lanes(part, part)
    share = jnp.sum(jnp.where(eye, product, 0.0), axis=0, keepdims=True)
    on_diag = lax.broadcasted_iota(jnp.int32, (part, part), 0) == lanes(part, part)
    own = rows_ref[:, pl.ds(pl.multiple_of(depth * part, part), part)].astype(F32)
    own = jnp.sum(jnp.where(on_diag, own, 0.0), axis=0, keepdims=True)
    twice = jnp.where(row == col, 2.0, 0.0) * own
    first = depth * (part // BLOCK)
    flags = jnp.where(lanes(1, part) < BLOCK, flag_ref[first], flag_ref[first + 1])
    share = jnp.where(flags == 1, share, twice - share)
    rows8 = lax.broadcasted_iota(jnp.int32, (8, part), 0)
    full = jnp.broadcast_to(share, (8, part))
    base = jnp.where(rows8 % 2 == 0, pltpu.roll(full, BLOCK, 1), full)
    high = base.astype(BF16).astype(F32)
    middle = (base - high).astype(BF16).astype(F32)
    low = (base - high - middle).astype(BF16).astype(F32)
    terms = jnp.where(rows8 < 2, high, jnp.where(rows8 < 4, middle, jnp.where(rows8 < 6, low, 0.0)))
    wide = total.shape[1]
    last = jnp.where(lanes(8, part) < BLOCK, total[:, wide - part :], terms)
    send = jnp.concatenate([total[:, : wide - part], last], axis=1).astype(BF16)
    for target in range(out_ref.shape[0]):
        out_ref[target] = send


def held_at(block_row, row, n_rows):
    owner = block_row // n_rows
    distance = (owner // 2 - row // 2) & 7
    place = (jnp.int32(PLACES) >> (distance * 4)) & 7
    place = place + ((owner ^ row) & 1) * 8
    return place * n_rows + block_row % n_rows


def from_chip(distance, value):
    n_row = lax.axis_size("row")
    return lax.ppermute(value, "row", [(s, (s - 2 * distance) % n_row) for s in range(n_row)])


def gather_strip(strip, across):
    n_row = lax.axis_size("row")
    pair = jnp.concatenate([strip, across], axis=0)
    above, below = from_chip(1, pair), from_chip(-1, pair)
    second, sixth = from_chip(2, strip), from_chip(-2, strip)
    held = jnp.concatenate([pair, second, sixth, above, below], axis=0)
    return held, lax.ppermute(held, "row", [(s, s ^ 1) for s in range(n_row)])


def product_kernel(
    ids_ref, pat_ref, flag_ref, count_ref, strip_ref, slots_ref, even_ref, odd_ref, out_ref, pop_ref, full, chosen
):
    row, col, depth = ids_ref[0], ids_ref[1], ids_ref[2]
    n_rows, names = pat_ref.shape
    width = strip_ref.shape[1]
    first_col = col * n_rows
    which = lanes(BLOCK, width) // BLOCK
    used = (names + 1) * BLOCK
    half = even_ref.shape[0]
    full[0:half, :] = even_ref[...]
    full[half : 2 * half, :] = odd_ref[...]
    for i in range(n_rows):
        bits = block_bits(pat_ref, i, row * n_rows + i, first_col, n_rows)
        keep = (lax.shift_right_logical(bits, depth * (width // BLOCK)) >> which) & 1
        chosen[i, used:, :] = jnp.zeros_like(chosen[i, used:, :])
        for slot in range(names + 1):
            listed = row * n_rows + i if slot == names else pat_ref[i, slot]
            source = pl.ds(pl.multiple_of(held_at(listed, row, n_rows) * BLOCK, BLOCK), BLOCK)
            chosen[i, slot * BLOCK : (slot + 1) * BLOCK, :] = full[source, :]
        here = pl.ds(i * BLOCK, BLOCK)
        squared = jnp.dot(slots_ref[here, :], chosen[i], preferred_element_type=F32)
        own = strip_ref[here, :].astype(F32)
        flag = jnp.broadcast_to(flag_ref[i], squared.shape)
        value = jnp.where(flag == 1, squared, 2.0 * own - squared)
        out_ref[here, :] = jnp.where(keep == 1, value, 0.0).astype(BF16)
    atoms = count_ref.shape[1]
    span = 2 * BLOCK
    wide = slots_ref.shape[1]
    low = lax.broadcasted_iota(jnp.int32, (atoms, atoms), 0)
    counts = jnp.broadcast_to(count_ref[...].astype(F32), (atoms, atoms))
    ends = jnp.sum(jnp.where(lanes(atoms, atoms) <= low, counts, 0.0), axis=1, keepdims=True)
    starts = jnp.sum(jnp.where(lanes(atoms, atoms) < low, counts, 0.0), axis=1, keepdims=True)
    at = lanes(atoms, span)
    total = jnp.zeros((atoms, span), F32)
    per_depth = 2 * BLOCK
    for d in range(n_rows // 2):
        terms = slots_ref[d * per_depth : (d + 1) * per_depth, wide - span :].astype(F32)
        terms = jnp.sum(terms.reshape(per_depth // 8, 8, span), axis=0)
        diag = terms[0:2] + terms[2:4] + terms[4:6]
        diag = diag.astype(BF16).astype(F32)
        for u in range(2):
            place = (at + ((2 * d + u) * BLOCK - BLOCK)).astype(F32)
            inside = (place >= starts) & (place < ends) & (at >= BLOCK)
            total = total + jnp.where(inside, jnp.broadcast_to(diag[u : u + 1], (atoms, span)), 0.0)
    ones = jnp.ones((8, span), F32)
    sums = lax.dot_general(
        ones, total, (((1,), (1,)), ((), ())), precision=lax.Precision.HIGHEST, preferred_element_type=F32
    )
    pop_ref[...] = sums[0:1]


def per_device(density, pattern, orbital_counts, branch_flag):
    tile = density.shape[0]
    n_row, n_col, n_depth = (lax.axis_size(name) for name in ("row", "col", "depth"))
    width = tile // n_depth
    n_rows, names = pattern.shape
    slots_wide = (names + 2) * BLOCK
    ids = jnp.stack([lax.axis_index("row"), lax.axis_index("col"), lax.axis_index("depth")]).astype(jnp.int32)
    limit = pltpu.CompilerParams(vmem_limit_bytes=24 << 20)
    strip, rows, slots = pl.pallas_call(
        pack_kernel,
        out_shape=(
            jax.ShapeDtypeStruct((tile, width), BF16),
            jax.ShapeDtypeStruct((width, tile), BF16),
            jax.ShapeDtypeStruct((width, slots_wide), BF16),
        ),
        in_specs=[SMEM, SMEM, VMEM],
        out_specs=(VMEM, VMEM, VMEM),
        scratch_shapes=[pltpu.VMEM((tile // BLOCK + 1, width, 2 * BLOCK), F32)],
        compiler_params=limit,
        name="pack",
    )(ids, pattern, density)
    across = from_chip(4, strip)
    swap = [(r * n_col + c, c * n_col + r) for r in range(n_row) for c in range(n_col)]
    trans = lax.ppermute(strip, ("row", "col"), swap)
    chunk = width // n_col
    parts = lax.all_to_all(slots.reshape(n_col, chunk, slots_wide), "col", 0, 0)
    trans, parts, across = lax.optimization_barrier((trans, parts, across))
    held, other = gather_strip(strip, across)
    send = pl.pallas_call(
        share_kernel,
        out_shape=jax.ShapeDtypeStruct((n_depth * n_col, chunk, slots_wide), BF16),
        in_specs=[SMEM, SMEM, VMEM, VMEM, VMEM],
        out_specs=VMEM,
        compiler_params=limit,
        name="share",
    )(ids, branch_flag, rows, trans, parts)
    stripe = lax.all_to_all(send, ("depth", "col"), 0, 0).reshape(tile, slots_wide)
    updated, populations = pl.pallas_call(
        product_kernel,
        out_shape=(
            jax.ShapeDtypeStruct((tile, width), BF16),
            jax.ShapeDtypeStruct((1, orbital_counts.shape[1]), F32),
        ),
        in_specs=[SMEM, SMEM, SMEM, VMEM, VMEM, VMEM, VMEM, VMEM],
        out_specs=(VMEM, VMEM),
        scratch_shapes=[
            pltpu.VMEM((n_row * tile, width), BF16),
            pltpu.VMEM((n_rows, slots_wide, width), BF16),
        ],
        compiler_params=limit,
        name="product",
    )(ids, pattern, branch_flag, orbital_counts, strip, stripe, held, other)
    return (updated, populations.reshape(-1))


def solution(mesh):
    in_specs = (P("row", "col"), P("row", None), P("row", None), P("row"))
    out_specs = (P("row", ("col", "depth")), P("row"))
    return jax.shard_map(
        per_device, mesh=mesh, in_specs=in_specs, out_specs=out_specs, check_vma=False
    )
```

```python
import functools

import jax
import jax.numpy as jnp
from jax import lax
from jax.experimental import pallas as pl
from jax.experimental.pallas import tpu as pltpu
from jax.sharding import PartitionSpec as P

BLOCK = 64
VMEM = pl.BlockSpec(memory_space=pltpu.VMEM)
SMEM = pl.BlockSpec(memory_space=pltpu.SMEM)
F32 = jnp.float32
BF16 = jnp.bfloat16
PLACES = 0x63517240
COST = 1 << 36


def lanes(rows, count):
    return lax.broadcasted_iota(jnp.int32, (rows, count), 1)


def block_bits(pat_ref, block_row, own_block, first_col, count):
    bits = jnp.int32(0)
    for slot in range(pat_ref.shape[1] + 1):
        listed = own_block if slot == pat_ref.shape[1] else pat_ref[block_row, slot]
        local = listed - first_col
        inside = (local >= 0) & (local < count)
        bits = bits | jnp.where(inside, jnp.int32(1) << jnp.clip(local, 0, count - 1), 0)
    return bits


def pack_kernel(ids_ref, pat_ref, dens_ref, strip_ref, rows_ref, slots_ref, blocks):
    row, col, depth = ids_ref[0], ids_ref[1], ids_ref[2]
    n_rows, names = pat_ref.shape
    tile = dens_ref.shape[1]
    n_cols = tile // BLOCK
    width = strip_ref.shape[1]
    part = rows_ref.shape[0]
    first_col = col * n_cols
    start = pl.multiple_of(depth * width, width)
    which = lanes(BLOCK, width) // BLOCK
    for i in range(n_rows):
        bits = block_bits(pat_ref, i, row * n_rows + i, first_col, n_cols)
        keep = (lax.shift_right_logical(bits, depth * (width // BLOCK)) >> which) & 1
        here = pl.ds(i * BLOCK, BLOCK)
        value = dens_ref[here, pl.ds(start, width)].astype(F32)
        strip_ref[here, :] = jnp.where(keep == 1, value, 0.0).astype(BF16)
    first_row = depth * (part // BLOCK)
    begin = pl.multiple_of(depth * part, part)
    which = lanes(BLOCK, tile) // BLOCK
    blocks[n_cols] = jnp.zeros_like(blocks[n_cols])
    for u in range(part // BLOCK):
        i = first_row + u
        bits = block_bits(pat_ref, i, row * n_rows + i, first_col, n_cols)
        value = dens_ref[pl.ds(pl.multiple_of(begin + u * BLOCK, BLOCK), BLOCK), :].astype(F32)
        value = jnp.where(((bits >> which) & 1) == 1, value, 0.0)
        here = pl.ds(u * BLOCK, BLOCK)
        rows_ref[here, :] = value.astype(BF16)
        for j in range(n_cols):
            one = value[:, j * BLOCK : (j + 1) * BLOCK]
            blocks[j, here, :] = jnp.concatenate([one, one], axis=1)
    left = lanes(BLOCK, 2 * BLOCK) < BLOCK
    for u in range(part // BLOCK):
        i = first_row + u
        own_block = row * n_rows + i
        here = pl.ds(u * BLOCK, BLOCK)
        places = []
        repeated = jnp.int32(0)
        for slot in range(names):
            listed = pat_ref[i, slot]
            local = listed - first_col
            places.append(jnp.where((local >= 0) & (local < n_cols), local, n_cols))
            repeated = repeated | jnp.where(listed == own_block, 1, 0)
        local = own_block - first_col
        inside = (local >= 0) & (local < n_cols) & (repeated == 0)
        places.append(jnp.where(inside, local, n_cols))
        places.append(jnp.int32(n_cols))
        for pair in range(len(places) // 2):
            value = jnp.where(
                left, blocks[places[2 * pair], here, :], blocks[places[2 * pair + 1], here, :]
            )
            slots_ref[here, pair * 2 * BLOCK : (pair + 1) * 2 * BLOCK] = value.astype(BF16)


def diagonal_kernel(ids_ref, flag_ref, rows_ref, trans_ref, terms_ref):
    row, col, depth = ids_ref[0], ids_ref[1], ids_ref[2]
    part = rows_ref.shape[0]
    product = jnp.dot(rows_ref[...], trans_ref[...], preferred_element_type=F32)
    eye = lax.broadcasted_iota(jnp.int32, (part, part), 0) == lanes(part, part)
    share = jnp.sum(jnp.where(eye, product, 0.0), axis=0, keepdims=True)
    own = rows_ref[:, pl.ds(pl.multiple_of(depth * part, part), part)].astype(F32)
    own = jnp.sum(jnp.where(eye, own, 0.0), axis=0, keepdims=True)
    twice = jnp.where(row == col, 2.0, 0.0) * own
    first = depth * (part // BLOCK)
    flags = jnp.where(lanes(1, part) < BLOCK, flag_ref[first], flag_ref[first + 1])
    share = jnp.where(flags == 1, share, twice - share)
    rows8 = lax.broadcasted_iota(jnp.int32, (8, part), 0)
    full = jnp.broadcast_to(share, (8, part))
    base = jnp.where(rows8 % 2 == 0, pltpu.roll(full, BLOCK, 1), full)
    high = base.astype(BF16).astype(F32)
    middle = (base - high).astype(BF16).astype(F32)
    low = (base - high - middle).astype(BF16).astype(F32)
    terms_ref[...] = jnp.where(rows8 < 2, high, jnp.where(rows8 < 4, middle, jnp.where(rows8 < 6, low, 0.0)))


def share_kernel(terms_ref, parts_ref, out_ref):
    total = parts_ref[0].astype(F32)
    for source in range(1, parts_ref.shape[0]):
        total = total + parts_ref[source].astype(F32)
    part = terms_ref.shape[1]
    wide = total.shape[1]
    last = jnp.where(lanes(8, part) < BLOCK, total[:, wide - part :], terms_ref[...])
    send = jnp.concatenate([total[:, : wide - part], last], axis=1).astype(BF16)
    for target in range(out_ref.shape[0]):
        out_ref[target] = send


def held_at(block_row, row, n_rows):
    owner = block_row // n_rows
    distance = (owner // 2 - row // 2) & 7
    place = (jnp.int32(PLACES) >> (distance * 4)) & 7
    place = place + ((owner ^ row) & 1) * 8
    return place * n_rows + block_row % n_rows


def from_chip(distance, value):
    n_row = lax.axis_size("row")
    return lax.ppermute(value, "row", [(s, (s - 2 * distance) % n_row) for s in range(n_row)])


def gather_strip(strip, across):
    n_row = lax.axis_size("row")
    pair = jnp.concatenate([strip, across], axis=0)
    above, below = from_chip(1, pair), from_chip(-1, pair)
    second, sixth = from_chip(2, strip), from_chip(-2, strip)
    held = jnp.concatenate([pair, second, sixth, above, below], axis=0)
    return held, lax.ppermute(held, "row", [(s, s ^ 1) for s in range(n_row)])


def product_kernel(
    ids_ref, pat_ref, flag_ref, count_ref, strip_ref, slots_ref, even_ref, odd_ref, out_ref, pop_ref, full, chosen
):
    row, col, depth = ids_ref[0], ids_ref[1], ids_ref[2]
    n_rows, names = pat_ref.shape
    width = strip_ref.shape[1]
    first_col = col * n_rows
    which = lanes(BLOCK, width) // BLOCK
    used = (names + 1) * BLOCK
    half = even_ref.shape[0]
    full[0:half, :] = even_ref[...]
    full[half : 2 * half, :] = odd_ref[...]
    for i in range(n_rows):
        bits = block_bits(pat_ref, i, row * n_rows + i, first_col, n_rows)
        keep = (lax.shift_right_logical(bits, depth * (width // BLOCK)) >> which) & 1
        chosen[i, used:, :] = jnp.zeros_like(chosen[i, used:, :])
        for slot in range(names + 1):
            listed = row * n_rows + i if slot == names else pat_ref[i, slot]
            source = pl.ds(pl.multiple_of(held_at(listed, row, n_rows) * BLOCK, BLOCK), BLOCK)
            chosen[i, slot * BLOCK : (slot + 1) * BLOCK, :] = full[source, :]
        here = pl.ds(i * BLOCK, BLOCK)
        squared = jnp.dot(slots_ref[here, :], chosen[i], preferred_element_type=F32)
        own = strip_ref[here, :].astype(F32)
        flag = jnp.broadcast_to(flag_ref[i], squared.shape)
        value = jnp.where(flag == 1, squared, 2.0 * own - squared)
        out_ref[here, :] = jnp.where(keep == 1, value, 0.0).astype(BF16)
    atoms = count_ref.shape[1]
    span = 2 * BLOCK
    wide = slots_ref.shape[1]
    low = lax.broadcasted_iota(jnp.int32, (atoms, atoms), 0)
    counts = jnp.broadcast_to(count_ref[...].astype(F32), (atoms, atoms))
    ends = jnp.sum(jnp.where(lanes(atoms, atoms) <= low, counts, 0.0), axis=1, keepdims=True)
    starts = jnp.sum(jnp.where(lanes(atoms, atoms) < low, counts, 0.0), axis=1, keepdims=True)
    at = lanes(atoms, span)
    total = jnp.zeros((atoms, span), F32)
    per_depth = 2 * BLOCK
    for d in range(n_rows // 2):
        terms = slots_ref[d * per_depth : (d + 1) * per_depth, wide - span :].astype(F32)
        terms = jnp.sum(terms.reshape(per_depth // 8, 8, span), axis=0)
        diag = terms[0:2] + terms[2:4] + terms[4:6]
        diag = diag.astype(BF16).astype(F32)
        for u in range(2):
            place = (at + ((2 * d + u) * BLOCK - BLOCK)).astype(F32)
            inside = (place >= starts) & (place < ends) & (at >= BLOCK)
            total = total + jnp.where(inside, jnp.broadcast_to(diag[u : u + 1], (atoms, span)), 0.0)
    ones = jnp.ones((8, span), F32)
    sums = lax.dot_general(
        ones, total, (((1,), (1,)), ((), ())), precision=lax.Precision.HIGHEST, preferred_element_type=F32
    )
    pop_ref[...] = sums[0:1]


def per_device(density, pattern, orbital_counts, branch_flag):
    tile = density.shape[0]
    n_row, n_col, n_depth = (lax.axis_size(name) for name in ("row", "col", "depth"))
    width = tile // n_depth
    n_rows, names = pattern.shape
    slots_wide = (names + 2) * BLOCK
    ids = jnp.stack([lax.axis_index("row"), lax.axis_index("col"), lax.axis_index("depth")]).astype(jnp.int32)
    limit = pltpu.CompilerParams(vmem_limit_bytes=24 << 20)
    strip, rows, slots = pl.pallas_call(
        pack_kernel,
        out_shape=(
            jax.ShapeDtypeStruct((tile, width), BF16),
            jax.ShapeDtypeStruct((width, tile), BF16),
            jax.ShapeDtypeStruct((width, slots_wide), BF16),
        ),
        in_specs=[SMEM, SMEM, VMEM],
        out_specs=(VMEM, VMEM, VMEM),
        scratch_shapes=[pltpu.VMEM((tile // BLOCK + 1, width, 2 * BLOCK), F32)],
        compiler_params=limit,
        name="pack",
    )(ids, pattern, density)
    across = from_chip(4, strip)
    swap = [(r * n_col + c, c * n_col + r) for r in range(n_row) for c in range(n_col)]
    trans = lax.ppermute(strip, ("row", "col"), swap)
    chunk = width // n_col
    parts = lax.all_to_all(slots.reshape(n_col, chunk, slots_wide), "col", 0, 0)
    parts, across = lax.optimization_barrier((parts, across))
    held, other = gather_strip(strip, across)
    terms = pl.pallas_call(
        diagonal_kernel,
        out_shape=jax.ShapeDtypeStruct((8, width), F32),
        in_specs=[SMEM, SMEM, VMEM, VMEM],
        out_specs=VMEM,
        compiler_params=limit,
        cost_estimate=pl.CostEstimate(flops=COST, bytes_accessed=1 << 20, transcendentals=0),
        name="diagonal",
    )(ids, branch_flag, rows, trans)
    send = pl.pallas_call(
        share_kernel,
        out_shape=jax.ShapeDtypeStruct((n_depth * n_col, chunk, slots_wide), BF16),
        in_specs=[VMEM, VMEM],
        out_specs=VMEM,
        compiler_params=limit,
        name="share",
    )(terms, parts)
    stripe = lax.all_to_all(send, ("depth", "col"), 0, 0).reshape(tile, slots_wide)
    updated, populations = pl.pallas_call(
        product_kernel,
        out_shape=(
            jax.ShapeDtypeStruct((tile, width), BF16),
            jax.ShapeDtypeStruct((1, orbital_counts.shape[1]), F32),
        ),
        in_specs=[SMEM, SMEM, SMEM, VMEM, VMEM, VMEM, VMEM, VMEM],
        out_specs=(VMEM, VMEM),
        scratch_shapes=[
            pltpu.VMEM((n_row * tile, width), BF16),
            pltpu.VMEM((n_rows, slots_wide, width), BF16),
        ],
        compiler_params=limit,
        name="product",
    )(ids, pattern, branch_flag, orbital_counts, strip, stripe, held, other)
    return (updated, populations.reshape(-1))


def solution(mesh):
    in_specs = (P("row", "col"), P("row", None), P("row", None), P("row"))
    out_specs = (P("row", ("col", "depth")), P("row"))
    return jax.shard_map(
        per_device, mesh=mesh, in_specs=in_specs, out_specs=out_specs, check_vma=False
    )
```

```python
import functools

import jax
import jax.numpy as jnp
from jax import lax
from jax.experimental import pallas as pl
from jax.experimental.pallas import tpu as pltpu
from jax.sharding import PartitionSpec as P

BLOCK = 64
VMEM = pl.BlockSpec(memory_space=pltpu.VMEM)
SMEM = pl.BlockSpec(memory_space=pltpu.SMEM)
HBM = pl.BlockSpec(memory_space=pltpu.HBM)
F32 = jnp.float32
BF16 = jnp.bfloat16
PLACES = 0x63517240
COST = 1 << 36


def lanes(rows, count):
    return lax.broadcasted_iota(jnp.int32, (rows, count), 1)


def block_bits(pat_ref, block_row, own_block, first_col, count):
    bits = jnp.int32(0)
    for slot in range(pat_ref.shape[1] + 1):
        listed = own_block if slot == pat_ref.shape[1] else pat_ref[block_row, slot]
        local = listed - first_col
        inside = (local >= 0) & (local < count)
        bits = bits | jnp.where(inside, jnp.int32(1) << jnp.clip(local, 0, count - 1), 0)
    return bits


def pack_kernel(pat_hbm, dens_hbm, strip_ref, rows_ref, slots_ref, pat_ref, dens_ref, blocks, done):
    pat_copy = pltpu.make_async_copy(pat_hbm, pat_ref, done.at[0])
    dens_copy = pltpu.make_async_copy(dens_hbm, dens_ref, done.at[1])
    pat_copy.start()
    dens_copy.start()
    row, col, depth = (lax.axis_index(name) for name in ("row", "col", "depth"))
    n_rows, names = pat_ref.shape
    tile = dens_ref.shape[1]
    n_cols = tile // BLOCK
    width = strip_ref.shape[1]
    part = rows_ref.shape[0]
    first_col = col * n_cols
    start = pl.multiple_of(depth * width, width)
    which = lanes(BLOCK, width) // BLOCK
    pat_copy.wait()
    kept = [block_bits(pat_ref, i, row * n_rows + i, first_col, n_cols) for i in range(n_rows)]
    dens_copy.wait()
    for i, bits in enumerate(kept):
        keep = (lax.shift_right_logical(bits, depth * (width // BLOCK)) >> which) & 1
        here = pl.ds(i * BLOCK, BLOCK)
        value = dens_ref[here, pl.ds(start, width)].astype(F32)
        strip_ref[here, :] = jnp.where(keep == 1, value, 0.0).astype(BF16)
    first_row = depth * (part // BLOCK)
    begin = pl.multiple_of(depth * part, part)
    which = lanes(BLOCK, tile) // BLOCK
    blocks[n_cols] = jnp.zeros_like(blocks[n_cols])
    for u in range(part // BLOCK):
        i = first_row + u
        bits = block_bits(pat_ref, i, row * n_rows + i, first_col, n_cols)
        value = dens_ref[pl.ds(pl.multiple_of(begin + u * BLOCK, BLOCK), BLOCK), :].astype(F32)
        value = jnp.where(((bits >> which) & 1) == 1, value, 0.0)
        here = pl.ds(u * BLOCK, BLOCK)
        rows_ref[here, :] = value.astype(BF16)
        for j in range(n_cols):
            one = value[:, j * BLOCK : (j + 1) * BLOCK]
            blocks[j, here, :] = jnp.concatenate([one, one], axis=1)
    left = lanes(BLOCK, 2 * BLOCK) < BLOCK
    for u in range(part // BLOCK):
        i = first_row + u
        own_block = row * n_rows + i
        here = pl.ds(u * BLOCK, BLOCK)
        places = []
        repeated = jnp.int32(0)
        for slot in range(names):
            listed = pat_ref[i, slot]
            local = listed - first_col
            places.append(jnp.where((local >= 0) & (local < n_cols), local, n_cols))
            repeated = repeated | jnp.where(listed == own_block, 1, 0)
        local = own_block - first_col
        inside = (local >= 0) & (local < n_cols) & (repeated == 0)
        places.append(jnp.where(inside, local, n_cols))
        places.append(jnp.int32(n_cols))
        for pair in range(len(places) // 2):
            value = jnp.where(
                left, blocks[places[2 * pair], here, :], blocks[places[2 * pair + 1], here, :]
            )
            slots_ref[here, pair * 2 * BLOCK : (pair + 1) * 2 * BLOCK] = value.astype(BF16)


def diagonal_kernel(rows_ref, trans_ref, terms_ref):
    row, col, depth = (lax.axis_index(name) for name in ("row", "col", "depth"))
    part = rows_ref.shape[0]
    product = jnp.dot(rows_ref[...], trans_ref[...], preferred_element_type=F32)
    eye = lax.broadcasted_iota(jnp.int32, (part, part), 0) == lanes(part, part)
    share = jnp.sum(jnp.where(eye, product, 0.0), axis=0, keepdims=True)
    own = rows_ref[:, pl.ds(pl.multiple_of(depth * part, part), part)].astype(F32)
    own = jnp.where(row == col, 1.0, 0.0) * jnp.sum(jnp.where(eye, own, 0.0), axis=0, keepdims=True)
    rows8 = lax.broadcasted_iota(jnp.int32, (8, part), 0)
    full = jnp.where(rows8 < 6, jnp.broadcast_to(share, (8, part)), jnp.broadcast_to(own, (8, part)))
    base = jnp.where(rows8 % 2 == 0, pltpu.roll(full, BLOCK, 1), full)
    high = base.astype(BF16).astype(F32)
    middle = (base - high).astype(BF16).astype(F32)
    low = (base - high - middle).astype(BF16).astype(F32)
    terms_ref[...] = jnp.where(rows8 < 2, high, jnp.where(rows8 < 4, middle, jnp.where(rows8 < 6, low, base)))


def share_kernel(terms_ref, parts_ref, out_ref):
    total = parts_ref[0].astype(F32)
    for source in range(1, parts_ref.shape[0]):
        total = total + parts_ref[source].astype(F32)
    part = terms_ref.shape[1]
    wide = total.shape[1]
    last = jnp.where(lanes(8, part) < BLOCK, total[:, wide - part :], terms_ref[...])
    send = jnp.concatenate([total[:, : wide - part], last], axis=1).astype(BF16)
    for target in range(out_ref.shape[0]):
        out_ref[target] = send


def held_at(block_row, row, n_rows):
    owner = block_row // n_rows
    distance = (owner // 2 - row // 2) & 7
    place = (jnp.int32(PLACES) >> (distance * 4)) & 7
    place = place + ((owner ^ row) & 1) * 8
    return place * n_rows + block_row % n_rows


def from_chip(distance, value):
    n_row = lax.axis_size("row")
    return lax.ppermute(value, "row", [(s, (s - 2 * distance) % n_row) for s in range(n_row)])


def gather_strip(strip, across):
    n_row = lax.axis_size("row")
    pair = jnp.concatenate([strip, across], axis=0)
    above, below = from_chip(1, pair), from_chip(-1, pair)
    second, sixth = from_chip(2, strip), from_chip(-2, strip)
    held = jnp.concatenate([pair, second, sixth, above, below], axis=0)
    return held, lax.ppermute(held, "row", [(s, s ^ 1) for s in range(n_row)])


def product_kernel(
    pat_ref, flag_ref, count_ref, strip_ref, slots_ref, even_ref, odd_ref, out_ref, pop_ref, full, chosen, done
):
    row, col, depth = (lax.axis_index(name) for name in ("row", "col", "depth"))
    n_rows, names = pat_ref.shape
    width = strip_ref.shape[1]
    first_col = col * n_rows
    which = lanes(BLOCK, width) // BLOCK
    used = (names + 1) * BLOCK
    half = even_ref.shape[0]
    even_copy = pltpu.make_async_copy(even_ref, full.at[pl.ds(0, half), :], done.at[0])
    odd_copy = pltpu.make_async_copy(odd_ref, full.at[pl.ds(half, half), :], done.at[1])
    even_copy.start()
    odd_copy.start()
    atoms = count_ref.shape[1]
    span = 2 * BLOCK
    wide = slots_ref.shape[1]
    low = lax.broadcasted_iota(jnp.int32, (atoms, atoms), 0)
    counts = jnp.broadcast_to(count_ref[...].astype(F32), (atoms, atoms))
    ends = jnp.sum(jnp.where(lanes(atoms, atoms) <= low, counts, 0.0), axis=1, keepdims=True)
    starts = jnp.sum(jnp.where(lanes(atoms, atoms) < low, counts, 0.0), axis=1, keepdims=True)
    at = lanes(atoms, span)
    total = jnp.zeros((atoms, span), F32)
    per_depth = 2 * BLOCK
    for d in range(n_rows // 2):
        terms = slots_ref[d * per_depth : (d + 1) * per_depth, wide - span :].astype(F32)
        terms = jnp.sum(terms.reshape(per_depth // 8, 8, span), axis=0)
        for u in range(2):
            squared = terms[u : u + 1] + terms[u + 2 : u + 3] + terms[u + 4 : u + 5]
            flag = jnp.broadcast_to(flag_ref[2 * d + u], squared.shape)
            diag = jnp.where(flag == 1, squared, 2.0 * terms[u + 6 : u + 7] - squared)
            diag = diag.astype(BF16).astype(F32)
            place = (at + ((2 * d + u) * BLOCK - BLOCK)).astype(F32)
            inside = (place >= starts) & (place < ends) & (at >= BLOCK)
            total = total + jnp.where(inside, jnp.broadcast_to(diag, (atoms, span)), 0.0)
    ones = jnp.ones((8, span), F32)
    sums = lax.dot_general(
        ones, total, (((1,), (1,)), ((), ())), precision=lax.Precision.HIGHEST, preferred_element_type=F32
    )
    pop_ref[...] = sums[0:1]
    even_copy.wait()
    odd_copy.wait()
    for i in range(n_rows):
        bits = block_bits(pat_ref, i, row * n_rows + i, first_col, n_rows)
        keep = (lax.shift_right_logical(bits, depth * (width // BLOCK)) >> which) & 1
        chosen[i, used:, :] = jnp.zeros_like(chosen[i, used:, :])
        for slot in range(names + 1):
            listed = row * n_rows + i if slot == names else pat_ref[i, slot]
            source = pl.ds(pl.multiple_of(held_at(listed, row, n_rows) * BLOCK, BLOCK), BLOCK)
            chosen[i, slot * BLOCK : (slot + 1) * BLOCK, :] = full[source, :]
        here = pl.ds(i * BLOCK, BLOCK)
        squared = jnp.dot(slots_ref[here, :], chosen[i], preferred_element_type=F32)
        own = strip_ref[here, :].astype(F32)
        flag = jnp.broadcast_to(flag_ref[i], squared.shape)
        value = jnp.where(flag == 1, squared, 2.0 * own - squared)
        out_ref[here, :] = jnp.where(keep == 1, value, 0.0).astype(BF16)


def per_device(density, pattern, orbital_counts, branch_flag):
    tile = density.shape[0]
    n_row, n_col, n_depth = (lax.axis_size(name) for name in ("row", "col", "depth"))
    width = tile // n_depth
    n_rows, names = pattern.shape
    slots_wide = (names + 2) * BLOCK
    limit = pltpu.CompilerParams(vmem_limit_bytes=24 << 20)
    strip, rows, slots = pl.pallas_call(
        pack_kernel,
        out_shape=(
            jax.ShapeDtypeStruct((tile, width), BF16),
            jax.ShapeDtypeStruct((width, tile), BF16),
            jax.ShapeDtypeStruct((width, slots_wide), BF16),
        ),
        in_specs=[HBM, HBM],
        out_specs=(VMEM, VMEM, VMEM),
        scratch_shapes=[
            pltpu.SMEM(pattern.shape, jnp.int32),
            pltpu.VMEM(density.shape, BF16),
            pltpu.VMEM((tile // BLOCK + 1, width, 2 * BLOCK), F32),
            pltpu.SemaphoreType.DMA((2,)),
        ],
        compiler_params=pltpu.CompilerParams(vmem_limit_bytes=60 << 20),
        name="pack",
    )(pattern, density)
    across = from_chip(4, strip)
    swap = [(r * n_col + c, c * n_col + r) for r in range(n_row) for c in range(n_col)]
    trans = lax.ppermute(strip, ("row", "col"), swap)
    chunk = width // n_col
    parts = lax.all_to_all(slots.reshape(n_col, chunk, slots_wide), "col", 0, 0)
    terms = pl.pallas_call(
        diagonal_kernel,
        out_shape=jax.ShapeDtypeStruct((8, width), F32),
        in_specs=[VMEM, VMEM],
        out_specs=VMEM,
        compiler_params=limit,
        cost_estimate=pl.CostEstimate(flops=COST, bytes_accessed=1 << 20, transcendentals=0),
        name="diagonal",
    )(rows, trans)
    send = pl.pallas_call(
        share_kernel,
        out_shape=jax.ShapeDtypeStruct((n_depth * n_col, chunk, slots_wide), BF16),
        in_specs=[VMEM, VMEM],
        out_specs=VMEM,
        compiler_params=limit,
        name="share",
    )(terms, parts)
    held, other = gather_strip(strip, across)
    stripe = lax.all_to_all(send, ("depth", "col"), 0, 0).reshape(tile, slots_wide)
    updated, populations = pl.pallas_call(
        product_kernel,
        out_shape=(
            jax.ShapeDtypeStruct((tile, width), BF16),
            jax.ShapeDtypeStruct((1, orbital_counts.shape[1]), F32),
        ),
        in_specs=[SMEM, SMEM, VMEM, VMEM, VMEM, VMEM, VMEM],
        out_specs=(VMEM, VMEM),
        scratch_shapes=[
            pltpu.VMEM((n_row * tile, width), BF16),
            pltpu.VMEM((n_rows, slots_wide, width), BF16),
            pltpu.SemaphoreType.DMA((2,)),
        ],
        compiler_params=limit,
        name="product",
    )(pattern, branch_flag, orbital_counts, strip, stripe, held, other)
    return (updated, populations.reshape(-1))


def solution(mesh):
    in_specs = (P("row", "col"), P("row", None), P("row", None), P("row"))
    out_specs = (P("row", ("col", "depth")), P("row"))
    return jax.shard_map(
        per_device, mesh=mesh, in_specs=in_specs, out_specs=out_specs, check_vma=False
    )
```

```python
import functools

import jax
import jax.numpy as jnp
from jax import lax
from jax.experimental import pallas as pl
from jax.experimental.pallas import tpu as pltpu
from jax.sharding import PartitionSpec as P

BLOCK = 64
VMEM = pl.BlockSpec(memory_space=pltpu.VMEM)
SMEM = pl.BlockSpec(memory_space=pltpu.SMEM)
HBM = pl.BlockSpec(memory_space=pltpu.HBM)
F32 = jnp.float32
BF16 = jnp.bfloat16
PLACES = 0x63517240
COST = int(5.3e9)


def lanes(rows, count):
    return lax.broadcasted_iota(jnp.int32, (rows, count), 1)


def block_bits(pat_ref, block_row, own_block, first_col, count):
    bits = jnp.int32(0)
    for slot in range(pat_ref.shape[1] + 1):
        listed = own_block if slot == pat_ref.shape[1] else pat_ref[block_row, slot]
        local = listed - first_col
        inside = (local >= 0) & (local < count)
        bits = bits | jnp.where(inside, jnp.int32(1) << jnp.clip(local, 0, count - 1), 0)
    return bits


def pack_kernel(pat_hbm, dens_hbm, strip_ref, rows_ref, slots_ref, pat_ref, dens_ref, blocks, done):
    pat_copy = pltpu.make_async_copy(pat_hbm, pat_ref, done.at[0])
    dens_copy = pltpu.make_async_copy(dens_hbm, dens_ref, done.at[1])
    pat_copy.start()
    dens_copy.start()
    row, col, depth = (lax.axis_index(name) for name in ("row", "col", "depth"))
    n_rows, names = pat_ref.shape
    tile = dens_ref.shape[1]
    n_cols = tile // BLOCK
    width = strip_ref.shape[1]
    part = rows_ref.shape[0]
    first_col = col * n_cols
    start = pl.multiple_of(depth * width, width)
    which = lanes(BLOCK, width) // BLOCK
    pat_copy.wait()
    kept = [block_bits(pat_ref, i, row * n_rows + i, first_col, n_cols) for i in range(n_rows)]
    dens_copy.wait()
    for i, bits in enumerate(kept):
        keep = (lax.shift_right_logical(bits, depth * (width // BLOCK)) >> which) & 1
        here = pl.ds(i * BLOCK, BLOCK)
        value = dens_ref[here, pl.ds(start, width)].astype(F32)
        strip_ref[here, :] = jnp.where(keep == 1, value, 0.0).astype(BF16)
    first_row = depth * (part // BLOCK)
    begin = pl.multiple_of(depth * part, part)
    which = lanes(BLOCK, tile) // BLOCK
    blocks[n_cols] = jnp.zeros_like(blocks[n_cols])
    for u in range(part // BLOCK):
        i = first_row + u
        bits = block_bits(pat_ref, i, row * n_rows + i, first_col, n_cols)
        value = dens_ref[pl.ds(pl.multiple_of(begin + u * BLOCK, BLOCK), BLOCK), :].astype(F32)
        value = jnp.where(((bits >> which) & 1) == 1, value, 0.0)
        here = pl.ds(u * BLOCK, BLOCK)
        rows_ref[here, :] = value.astype(BF16)
        for j in range(n_cols):
            one = value[:, j * BLOCK : (j + 1) * BLOCK]
            blocks[j, here, :] = jnp.concatenate([one, one], axis=1)
    left = lanes(BLOCK, 2 * BLOCK) < BLOCK
    for u in range(part // BLOCK):
        i = first_row + u
        own_block = row * n_rows + i
        here = pl.ds(u * BLOCK, BLOCK)
        places = []
        repeated = jnp.int32(0)
        for slot in range(names):
            listed = pat_ref[i, slot]
            local = listed - first_col
            places.append(jnp.where((local >= 0) & (local < n_cols), local, n_cols))
            repeated = repeated | jnp.where(listed == own_block, 1, 0)
        local = own_block - first_col
        inside = (local >= 0) & (local < n_cols) & (repeated == 0)
        places.append(jnp.where(inside, local, n_cols))
        places.append(jnp.int32(n_cols))
        for pair in range(len(places) // 2):
            value = jnp.where(
                left, blocks[places[2 * pair], here, :], blocks[places[2 * pair + 1], here, :]
            )
            slots_ref[here, pair * 2 * BLOCK : (pair + 1) * 2 * BLOCK] = value.astype(BF16)


def diagonal_kernel(rows_ref, trans_ref, terms_ref):
    row, col, depth = (lax.axis_index(name) for name in ("row", "col", "depth"))
    part = rows_ref.shape[0]
    product = jnp.dot(rows_ref[...], trans_ref[...], preferred_element_type=F32)
    eye = lax.broadcasted_iota(jnp.int32, (part, part), 0) == lanes(part, part)
    share = jnp.sum(jnp.where(eye, product, 0.0), axis=0, keepdims=True)
    own = rows_ref[:, pl.ds(pl.multiple_of(depth * part, part), part)].astype(F32)
    own = jnp.where(row == col, 1.0, 0.0) * jnp.sum(jnp.where(eye, own, 0.0), axis=0, keepdims=True)
    rows8 = lax.broadcasted_iota(jnp.int32, (8, part), 0)
    full = jnp.where(rows8 < 6, jnp.broadcast_to(share, (8, part)), jnp.broadcast_to(own, (8, part)))
    base = jnp.where(rows8 % 2 == 0, pltpu.roll(full, BLOCK, 1), full)
    high = base.astype(BF16).astype(F32)
    middle = (base - high).astype(BF16).astype(F32)
    low = (base - high - middle).astype(BF16).astype(F32)
    terms_ref[...] = jnp.where(rows8 < 2, high, jnp.where(rows8 < 4, middle, jnp.where(rows8 < 6, low, base)))


def share_kernel(terms_ref, parts_ref, out_ref):
    total = parts_ref[0].astype(F32)
    for source in range(1, parts_ref.shape[0]):
        total = total + parts_ref[source].astype(F32)
    part = terms_ref.shape[1]
    wide = total.shape[1]
    last = jnp.where(lanes(8, part) < BLOCK, total[:, wide - part :], terms_ref[...])
    send = jnp.concatenate([total[:, : wide - part], last], axis=1).astype(BF16)
    for target in range(out_ref.shape[0]):
        out_ref[target] = send


def held_at(block_row, row, n_rows):
    owner = block_row // n_rows
    distance = (owner // 2 - row // 2) & 7
    place = (jnp.int32(PLACES) >> (distance * 4)) & 7
    place = place + ((owner ^ row) & 1) * 8
    return place * n_rows + block_row % n_rows


def from_chip(distance, value):
    n_row = lax.axis_size("row")
    return lax.ppermute(value, "row", [(s, (s - 2 * distance) % n_row) for s in range(n_row)])


def gather_strip(strip, across):
    n_row = lax.axis_size("row")
    pair = jnp.concatenate([strip, across], axis=0)
    above, below = from_chip(1, pair), from_chip(-1, pair)
    second, sixth = from_chip(2, strip), from_chip(-2, strip)
    held = jnp.concatenate([pair, second, sixth, above, below], axis=0)
    return held, lax.ppermute(held, "row", [(s, s ^ 1) for s in range(n_row)])


def product_kernel(
    pat_ref, flag_ref, count_ref, strip_ref, slots_ref, even_ref, odd_ref, out_ref, pop_ref, full, chosen, done
):
    row, col, depth = (lax.axis_index(name) for name in ("row", "col", "depth"))
    n_rows, names = pat_ref.shape
    width = strip_ref.shape[1]
    first_col = col * n_rows
    which = lanes(BLOCK, width) // BLOCK
    used = (names + 1) * BLOCK
    half = even_ref.shape[0]
    even_copy = pltpu.make_async_copy(even_ref, full.at[pl.ds(0, half), :], done.at[0])
    odd_copy = pltpu.make_async_copy(odd_ref, full.at[pl.ds(half, half), :], done.at[1])
    even_copy.start()
    odd_copy.start()
    atoms = count_ref.shape[1]
    span = 2 * BLOCK
    wide = slots_ref.shape[1]
    low = lax.broadcasted_iota(jnp.int32, (atoms, atoms), 0)
    counts = jnp.broadcast_to(count_ref[...].astype(F32), (atoms, atoms))
    ends = jnp.sum(jnp.where(lanes(atoms, atoms) <= low, counts, 0.0), axis=1, keepdims=True)
    starts = jnp.sum(jnp.where(lanes(atoms, atoms) < low, counts, 0.0), axis=1, keepdims=True)
    at = lanes(atoms, span)
    total = jnp.zeros((atoms, span), F32)
    per_depth = 2 * BLOCK
    for d in range(n_rows // 2):
        terms = slots_ref[d * per_depth : (d + 1) * per_depth, wide - span :].astype(F32)
        terms = jnp.sum(terms.reshape(per_depth // 8, 8, span), axis=0)
        for u in range(2):
            squared = terms[u : u + 1] + terms[u + 2 : u + 3] + terms[u + 4 : u + 5]
            flag = jnp.broadcast_to(flag_ref[2 * d + u], squared.shape)
            diag = jnp.where(flag == 1, squared, 2.0 * terms[u + 6 : u + 7] - squared)
            diag = diag.astype(BF16).astype(F32)
            place = (at + ((2 * d + u) * BLOCK - BLOCK)).astype(F32)
            inside = (place >= starts) & (place < ends) & (at >= BLOCK)
            total = total + jnp.where(inside, jnp.broadcast_to(diag, (atoms, span)), 0.0)
    ones = jnp.ones((8, span), F32)
    sums = lax.dot_general(
        ones, total, (((1,), (1,)), ((), ())), precision=lax.Precision.HIGHEST, preferred_element_type=F32
    )
    pop_ref[...] = sums[0:1]
    even_copy.wait()
    odd_copy.wait()
    for i in range(n_rows):
        bits = block_bits(pat_ref, i, row * n_rows + i, first_col, n_rows)
        keep = (lax.shift_right_logical(bits, depth * (width // BLOCK)) >> which) & 1
        chosen[i, used:, :] = jnp.zeros_like(chosen[i, used:, :])
        for slot in range(names + 1):
            listed = row * n_rows + i if slot == names else pat_ref[i, slot]
            source = pl.ds(pl.multiple_of(held_at(listed, row, n_rows) * BLOCK, BLOCK), BLOCK)
            chosen[i, slot * BLOCK : (slot + 1) * BLOCK, :] = full[source, :]
        here = pl.ds(i * BLOCK, BLOCK)
        squared = jnp.dot(slots_ref[here, :], chosen[i], preferred_element_type=F32)
        own = strip_ref[here, :].astype(F32)
        flag = jnp.broadcast_to(flag_ref[i], squared.shape)
        value = jnp.where(flag == 1, squared, 2.0 * own - squared)
        out_ref[here, :] = jnp.where(keep == 1, value, 0.0).astype(BF16)


def per_device(density, pattern, orbital_counts, branch_flag):
    tile = density.shape[0]
    n_row, n_col, n_depth = (lax.axis_size(name) for name in ("row", "col", "depth"))
    width = tile // n_depth
    n_rows, names = pattern.shape
    slots_wide = (names + 2) * BLOCK
    limit = pltpu.CompilerParams(vmem_limit_bytes=24 << 20)
    strip, rows, slots = pl.pallas_call(
        pack_kernel,
        out_shape=(
            jax.ShapeDtypeStruct((tile, width), BF16),
            jax.ShapeDtypeStruct((width, tile), BF16),
            jax.ShapeDtypeStruct((width, slots_wide), BF16),
        ),
        in_specs=[HBM, HBM],
        out_specs=(VMEM, VMEM, VMEM),
        scratch_shapes=[
            pltpu.SMEM(pattern.shape, jnp.int32),
            pltpu.VMEM(density.shape, BF16),
            pltpu.VMEM((tile // BLOCK + 1, width, 2 * BLOCK), F32),
            pltpu.SemaphoreType.DMA((2,)),
        ],
        compiler_params=pltpu.CompilerParams(vmem_limit_bytes=60 << 20),
        name="pack",
    )(pattern, density)
    swap = [(r * n_col + c, c * n_col + r) for r in range(n_row) for c in range(n_col)]
    trans = lax.ppermute(strip, ("row", "col"), swap)
    chunk = width // n_col
    parts = lax.all_to_all(slots.reshape(n_col, chunk, slots_wide), "col", 0, 0)
    across = from_chip(4, strip)
    terms = pl.pallas_call(
        diagonal_kernel,
        out_shape=jax.ShapeDtypeStruct((8, width), F32),
        in_specs=[VMEM, VMEM],
        out_specs=VMEM,
        compiler_params=limit,
        cost_estimate=pl.CostEstimate(flops=COST, bytes_accessed=1 << 20, transcendentals=0),
        name="diagonal",
    )(rows, trans)
    send = pl.pallas_call(
        share_kernel,
        out_shape=jax.ShapeDtypeStruct((n_depth * n_col, chunk, slots_wide), BF16),
        in_specs=[VMEM, VMEM],
        out_specs=VMEM,
        compiler_params=limit,
        name="share",
    )(terms, parts)
    send, across = lax.optimization_barrier((send, across))
    held, other = gather_strip(strip, across)
    stripe = lax.all_to_all(send, ("depth", "col"), 0, 0).reshape(tile, slots_wide)
    updated, populations = pl.pallas_call(
        product_kernel,
        out_shape=(
            jax.ShapeDtypeStruct((tile, width), BF16),
            jax.ShapeDtypeStruct((1, orbital_counts.shape[1]), F32),
        ),
        in_specs=[SMEM, SMEM, VMEM, VMEM, VMEM, VMEM, VMEM],
        out_specs=(VMEM, VMEM),
        scratch_shapes=[
            pltpu.VMEM((n_row * tile, width), BF16),
            pltpu.VMEM((n_rows, slots_wide, width), BF16),
            pltpu.SemaphoreType.DMA((2,)),
        ],
        compiler_params=limit,
        name="product",
    )(pattern, branch_flag, orbital_counts, strip, stripe, held, other)
    return (updated, populations.reshape(-1))


def solution(mesh):
    in_specs = (P("row", "col"), P("row", None), P("row", None), P("row"))
    out_specs = (P("row", ("col", "depth")), P("row"))
    return jax.shard_map(
        per_device, mesh=mesh, in_specs=in_specs, out_specs=out_specs, check_vma=False
    )
```

```python
import functools

import jax
import jax.numpy as jnp
from jax import lax
from jax.experimental import pallas as pl
from jax.experimental.pallas import tpu as pltpu
from jax.sharding import PartitionSpec as P

BLOCK = 64
VMEM = pl.BlockSpec(memory_space=pltpu.VMEM)
SMEM = pl.BlockSpec(memory_space=pltpu.SMEM)
HBM = pl.BlockSpec(memory_space=pltpu.HBM)
F32 = jnp.float32
BF16 = jnp.bfloat16
GROUP = 4
PLACES = 0x63517240
COST = int(5.3e9)


def lanes(rows, count):
    return lax.broadcasted_iota(jnp.int32, (rows, count), 1)


def block_bits(pat_ref, block_row, own_block, first_col, count):
    bits = jnp.int32(0)
    for slot in range(pat_ref.shape[1] + 1):
        listed = own_block if slot == pat_ref.shape[1] else pat_ref[block_row, slot]
        local = listed - first_col
        inside = (local >= 0) & (local < count)
        bits = bits | jnp.where(inside, jnp.int32(1) << jnp.clip(local, 0, count - 1), 0)
    return bits


def pack_kernel(pat_hbm, dens_hbm, strip_ref, rows_ref, slots_ref, pat_ref, dens_ref, blocks, done):
    pat_copy = pltpu.make_async_copy(pat_hbm, pat_ref, done.at[0])
    dens_copy = pltpu.make_async_copy(dens_hbm, dens_ref, done.at[1])
    pat_copy.start()
    dens_copy.start()
    row, col, depth = (lax.axis_index(name) for name in ("row", "col", "depth"))
    n_rows, names = pat_ref.shape
    tile = dens_ref.shape[1]
    n_cols = tile // BLOCK
    width = strip_ref.shape[1]
    part = rows_ref.shape[0]
    first_col = col * n_cols
    start = pl.multiple_of(depth * width, width)
    which = lanes(BLOCK, width) // BLOCK
    pat_copy.wait()
    kept = [block_bits(pat_ref, i, row * n_rows + i, first_col, n_cols) for i in range(n_rows)]
    dens_copy.wait()
    for i, bits in enumerate(kept):
        keep = (lax.shift_right_logical(bits, depth * (width // BLOCK)) >> which) & 1
        here = pl.ds(i * BLOCK, BLOCK)
        value = dens_ref[here, pl.ds(start, width)].astype(F32)
        strip_ref[here, :] = jnp.where(keep == 1, value, 0.0).astype(BF16)
    first_row = depth * (part // BLOCK)
    begin = pl.multiple_of(depth * part, part)
    which = lanes(BLOCK, tile) // BLOCK
    blocks[n_cols] = jnp.zeros_like(blocks[n_cols])
    for u in range(part // BLOCK):
        i = first_row + u
        bits = block_bits(pat_ref, i, row * n_rows + i, first_col, n_cols)
        value = dens_ref[pl.ds(pl.multiple_of(begin + u * BLOCK, BLOCK), BLOCK), :].astype(F32)
        value = jnp.where(((bits >> which) & 1) == 1, value, 0.0)
        here = pl.ds(u * BLOCK, BLOCK)
        rows_ref[here, :] = value.astype(BF16)
        for j in range(n_cols):
            one = value[:, j * BLOCK : (j + 1) * BLOCK]
            blocks[j, here, :] = jnp.concatenate([one, one], axis=1)
    left = lanes(BLOCK, 2 * BLOCK) < BLOCK
    for u in range(part // BLOCK):
        i = first_row + u
        own_block = row * n_rows + i
        here = pl.ds(u * BLOCK, BLOCK)
        places = []
        repeated = jnp.int32(0)
        for slot in range(names):
            listed = pat_ref[i, slot]
            local = listed - first_col
            places.append(jnp.where((local >= 0) & (local < n_cols), local, n_cols))
            repeated = repeated | jnp.where(listed == own_block, 1, 0)
        local = own_block - first_col
        inside = (local >= 0) & (local < n_cols) & (repeated == 0)
        places.append(jnp.where(inside, local, n_cols))
        places.append(jnp.int32(n_cols))
        for pair in range(len(places) // 2):
            value = jnp.where(
                left, blocks[places[2 * pair], here, :], blocks[places[2 * pair + 1], here, :]
            )
            slots_ref[here, pair * 2 * BLOCK : (pair + 1) * 2 * BLOCK] = value.astype(BF16)


def diagonal_kernel(rows_ref, trans_ref, terms_ref):
    row, col, depth = (lax.axis_index(name) for name in ("row", "col", "depth"))
    part = rows_ref.shape[0]
    product = jnp.dot(rows_ref[...], trans_ref[...], preferred_element_type=F32)
    eye = lax.broadcasted_iota(jnp.int32, (part, part), 0) == lanes(part, part)
    share = jnp.sum(jnp.where(eye, product, 0.0), axis=0, keepdims=True)
    own = rows_ref[:, pl.ds(pl.multiple_of(depth * part, part), part)].astype(F32)
    own = jnp.where(row == col, 1.0, 0.0) * jnp.sum(jnp.where(eye, own, 0.0), axis=0, keepdims=True)
    rows8 = lax.broadcasted_iota(jnp.int32, (8, part), 0)
    full = jnp.where(rows8 < 6, jnp.broadcast_to(share, (8, part)), jnp.broadcast_to(own, (8, part)))
    base = jnp.where(rows8 % 2 == 0, pltpu.roll(full, BLOCK, 1), full)
    high = base.astype(BF16).astype(F32)
    middle = (base - high).astype(BF16).astype(F32)
    low = (base - high - middle).astype(BF16).astype(F32)
    terms_ref[...] = jnp.where(rows8 < 2, high, jnp.where(rows8 < 4, middle, jnp.where(rows8 < 6, low, base)))


def share_kernel(terms_ref, parts_ref, out_ref):
    total = parts_ref[0].astype(F32)
    for source in range(1, parts_ref.shape[0]):
        total = total + parts_ref[source].astype(F32)
    part = terms_ref.shape[1]
    wide = total.shape[1]
    last = jnp.where(lanes(8, part) < BLOCK, total[:, wide - part :], terms_ref[...])
    send = jnp.concatenate([total[:, : wide - part], last], axis=1).astype(BF16)
    for target in range(out_ref.shape[0]):
        out_ref[target] = send


def held_at(block_row, row, n_rows):
    owner = block_row // n_rows
    distance = (owner // 2 - row // 2) & 7
    place = (jnp.int32(PLACES) >> (distance * 4)) & 7
    place = place + ((owner ^ row) & 1) * 8
    return place * n_rows + block_row % n_rows


def from_chip(distance, value):
    n_row = lax.axis_size("row")
    return lax.ppermute(value, "row", [(s, (s - 2 * distance) % n_row) for s in range(n_row)])


def gather_strip(strip, across):
    n_row = lax.axis_size("row")
    pair = jnp.concatenate([strip, across], axis=0)
    above, below = from_chip(1, pair), from_chip(-1, pair)
    second, sixth = from_chip(2, strip), from_chip(-2, strip)
    held = jnp.concatenate([pair, second, sixth, above, below], axis=0)
    return held, lax.ppermute(held, "row", [(s, s ^ 1) for s in range(n_row)])


def plan_kernel(pat_ref, _, plan_ref):
    row, col, depth = (lax.axis_index(name) for name in ("row", "col", "depth"))
    n_rows, names = pat_ref.shape
    blocks = n_rows // lax.axis_size("depth")
    for i in range(n_rows):
        own_block = row * n_rows + i
        for slot in range(names + 1):
            listed = own_block if slot == names else pat_ref[i, slot]
            plan_ref[i, slot] = held_at(listed, row, n_rows) * BLOCK
        plan_ref[i, names + 1] = block_bits(pat_ref, i, own_block, col * n_rows + depth * blocks, blocks)


def product_kernel(
    plan_ref, flag_ref, count_ref, strip_ref, slots_ref, even_ref, odd_ref, out_ref, pop_ref, full
):
    n_rows, slots = plan_ref.shape[0], plan_ref.shape[1] - 1
    width = strip_ref.shape[1]
    which = lanes(BLOCK, width) // BLOCK
    half = even_ref.shape[0]
    full[0:half, :] = even_ref[...]
    full[half : 2 * half, :] = odd_ref[...]
    atoms = count_ref.shape[1]
    span = 2 * BLOCK
    wide = slots_ref.shape[1]
    low = lax.broadcasted_iota(jnp.int32, (atoms, atoms), 0)
    counts = jnp.broadcast_to(count_ref[...].astype(F32), (atoms, atoms))
    ends = jnp.sum(jnp.where(lanes(atoms, atoms) <= low, counts, 0.0), axis=1, keepdims=True)
    starts = jnp.sum(jnp.where(lanes(atoms, atoms) < low, counts, 0.0), axis=1, keepdims=True)
    at = lanes(atoms, span)
    total = jnp.zeros((atoms, span), F32)
    per_depth = 2 * BLOCK
    for d in range(n_rows // 2):
        terms = slots_ref[d * per_depth : (d + 1) * per_depth, wide - span :].astype(F32)
        terms = jnp.sum(terms.reshape(per_depth // 8, 8, span), axis=0)
        for u in range(2):
            squared = terms[u : u + 1] + terms[u + 2 : u + 3] + terms[u + 4 : u + 5]
            flag = jnp.broadcast_to(flag_ref[2 * d + u], squared.shape)
            diag = jnp.where(flag == 1, squared, 2.0 * terms[u + 6 : u + 7] - squared)
            diag = diag.astype(BF16).astype(F32)
            place = (at + ((2 * d + u) * BLOCK - BLOCK)).astype(F32)
            inside = (place >= starts) & (place < ends) & (at >= BLOCK)
            total = total + jnp.where(inside, jnp.broadcast_to(diag, (atoms, span)), 0.0)
    ones = jnp.ones((8, span), F32)
    sums = lax.dot_general(
        ones, total, (((1,), (1,)), ((), ())), precision=lax.Precision.HIGHEST, preferred_element_type=F32
    )
    pop_ref[...] = sums[0:1]
    for i in range(n_rows):
        here = pl.ds(i * BLOCK, BLOCK)
        squared = jnp.zeros((BLOCK, width), F32)
        for first in range(0, slots, GROUP):
            last = min(first + GROUP, slots)
            starts = [pl.multiple_of(plan_ref[i, slot], BLOCK) for slot in range(first, last)]
            chosen = jnp.concatenate([full[pl.ds(start, BLOCK), :] for start in starts], axis=0)
            values = slots_ref[here, first * BLOCK : last * BLOCK]
            squared = squared + jnp.dot(values, chosen, preferred_element_type=F32)
        keep = (plan_ref[i, slots] >> which) & 1
        own = strip_ref[here, :].astype(F32)
        flag = jnp.broadcast_to(flag_ref[i], squared.shape)
        value = jnp.where(flag == 1, squared, 2.0 * own - squared)
        out_ref[here, :] = jnp.where(keep == 1, value, 0.0).astype(BF16)


def per_device(density, pattern, orbital_counts, branch_flag):
    tile = density.shape[0]
    n_row, n_col, n_depth = (lax.axis_size(name) for name in ("row", "col", "depth"))
    width = tile // n_depth
    n_rows, names = pattern.shape
    slots_wide = (names + 2) * BLOCK
    limit = pltpu.CompilerParams(vmem_limit_bytes=24 << 20)
    strip, rows, slots = pl.pallas_call(
        pack_kernel,
        out_shape=(
            jax.ShapeDtypeStruct((tile, width), BF16),
            jax.ShapeDtypeStruct((width, tile), BF16),
            jax.ShapeDtypeStruct((width, slots_wide), BF16),
        ),
        in_specs=[HBM, HBM],
        out_specs=(VMEM, VMEM, VMEM),
        scratch_shapes=[
            pltpu.SMEM(pattern.shape, jnp.int32),
            pltpu.VMEM(density.shape, BF16),
            pltpu.VMEM((tile // BLOCK + 1, width, 2 * BLOCK), F32),
            pltpu.SemaphoreType.DMA((2,)),
        ],
        compiler_params=pltpu.CompilerParams(vmem_limit_bytes=60 << 20),
        name="pack",
    )(pattern, density)
    swap = [(r * n_col + c, c * n_col + r) for r in range(n_row) for c in range(n_col)]
    trans = lax.ppermute(strip, ("row", "col"), swap)
    chunk = width // n_col
    parts = lax.all_to_all(slots.reshape(n_col, chunk, slots_wide), "col", 0, 0)
    across = from_chip(4, strip)
    terms = pl.pallas_call(
        diagonal_kernel,
        out_shape=jax.ShapeDtypeStruct((8, width), F32),
        in_specs=[VMEM, VMEM],
        out_specs=VMEM,
        compiler_params=limit,
        cost_estimate=pl.CostEstimate(flops=COST, bytes_accessed=1 << 20, transcendentals=0),
        name="diagonal",
    )(rows, trans)
    send = pl.pallas_call(
        share_kernel,
        out_shape=jax.ShapeDtypeStruct((n_depth * n_col, chunk, slots_wide), BF16),
        in_specs=[VMEM, VMEM],
        out_specs=VMEM,
        compiler_params=limit,
        name="share",
    )(terms, parts)
    send, across = lax.optimization_barrier((send, across))
    held, other = gather_strip(strip, across)
    stripe = lax.all_to_all(send, ("depth", "col"), 0, 0).reshape(tile, slots_wide)
    plan = pl.pallas_call(
        plan_kernel,
        out_shape=jax.ShapeDtypeStruct((n_rows, names + 2), jnp.int32),
        in_specs=[SMEM, pl.BlockSpec(memory_space=pl.ANY)],
        out_specs=SMEM,
        compiler_params=limit,
        cost_estimate=pl.CostEstimate(flops=1 << 31, bytes_accessed=1 << 12, transcendentals=0),
        name="plan",
    )(pattern, across)
    updated, populations = pl.pallas_call(
        product_kernel,
        out_shape=(
            jax.ShapeDtypeStruct((tile, width), BF16),
            jax.ShapeDtypeStruct((1, orbital_counts.shape[1]), F32),
        ),
        in_specs=[SMEM, SMEM, VMEM, VMEM, VMEM, VMEM, VMEM],
        out_specs=(VMEM, VMEM),
        scratch_shapes=[pltpu.VMEM((n_row * tile, width), BF16)],
        compiler_params=limit,
        name="product",
    )(plan, branch_flag, orbital_counts, strip, stripe, held, other)
    return (updated, populations.reshape(-1))


def solution(mesh):
    in_specs = (P("row", "col"), P("row", None), P("row", None), P("row"))
    out_specs = (P("row", ("col", "depth")), P("row"))
    return jax.shard_map(
        per_device, mesh=mesh, in_specs=in_specs, out_specs=out_specs, check_vma=False
    )
```

```python
import functools

import jax
import jax.numpy as jnp
from jax import lax
from jax.experimental import pallas as pl
from jax.experimental.pallas import tpu as pltpu
from jax.sharding import PartitionSpec as P

BLOCK = 64
VMEM = pl.BlockSpec(memory_space=pltpu.VMEM)
SMEM = pl.BlockSpec(memory_space=pltpu.SMEM)
HBM = pl.BlockSpec(memory_space=pltpu.HBM)
F32 = jnp.float32
BF16 = jnp.bfloat16
GROUP = 4
PLACES = 0x63517240
COST = int(5.3e9)
PAIR_COST = 1 << 33


def lanes(rows, count):
    return lax.broadcasted_iota(jnp.int32, (rows, count), 1)


def block_bits(pat_ref, block_row, own_block, first_col, count):
    bits = jnp.int32(0)
    for slot in range(pat_ref.shape[1] + 1):
        listed = own_block if slot == pat_ref.shape[1] else pat_ref[block_row, slot]
        local = listed - first_col
        inside = (local >= 0) & (local < count)
        bits = bits | jnp.where(inside, jnp.int32(1) << jnp.clip(local, 0, count - 1), 0)
    return bits


def pack_kernel(pat_hbm, dens_hbm, strip_ref, rows_ref, slots_ref, pat_ref, dens_ref, blocks, done):
    pat_copy = pltpu.make_async_copy(pat_hbm, pat_ref, done.at[0])
    dens_copy = pltpu.make_async_copy(dens_hbm, dens_ref, done.at[1])
    pat_copy.start()
    dens_copy.start()
    row, col, depth = (lax.axis_index(name) for name in ("row", "col", "depth"))
    n_rows, names = pat_ref.shape
    tile = dens_ref.shape[1]
    n_cols = tile // BLOCK
    width = strip_ref.shape[1]
    part = rows_ref.shape[0]
    first_col = col * n_cols
    start = pl.multiple_of(depth * width, width)
    which = lanes(BLOCK, width) // BLOCK
    pat_copy.wait()
    kept = [block_bits(pat_ref, i, row * n_rows + i, first_col, n_cols) for i in range(n_rows)]
    dens_copy.wait()
    for i, bits in enumerate(kept):
        keep = (lax.shift_right_logical(bits, depth * (width // BLOCK)) >> which) & 1
        here = pl.ds(i * BLOCK, BLOCK)
        value = dens_ref[here, pl.ds(start, width)].astype(F32)
        strip_ref[here, :] = jnp.where(keep == 1, value, 0.0).astype(BF16)
    first_row = depth * (part // BLOCK)
    begin = pl.multiple_of(depth * part, part)
    which = lanes(BLOCK, tile) // BLOCK
    blocks[n_cols] = jnp.zeros_like(blocks[n_cols])
    for u in range(part // BLOCK):
        i = first_row + u
        bits = block_bits(pat_ref, i, row * n_rows + i, first_col, n_cols)
        value = dens_ref[pl.ds(pl.multiple_of(begin + u * BLOCK, BLOCK), BLOCK), :].astype(F32)
        value = jnp.where(((bits >> which) & 1) == 1, value, 0.0)
        here = pl.ds(u * BLOCK, BLOCK)
        rows_ref[here, :] = value.astype(BF16)
        for j in range(n_cols):
            one = value[:, j * BLOCK : (j + 1) * BLOCK]
            blocks[j, here, :] = jnp.concatenate([one, one], axis=1)
    left = lanes(BLOCK, 2 * BLOCK) < BLOCK
    for u in range(part // BLOCK):
        i = first_row + u
        own_block = row * n_rows + i
        here = pl.ds(u * BLOCK, BLOCK)
        places = []
        repeated = jnp.int32(0)
        for slot in range(names):
            listed = pat_ref[i, slot]
            local = listed - first_col
            places.append(jnp.where((local >= 0) & (local < n_cols), local, n_cols))
            repeated = repeated | jnp.where(listed == own_block, 1, 0)
        local = own_block - first_col
        inside = (local >= 0) & (local < n_cols) & (repeated == 0)
        places.append(jnp.where(inside, local, n_cols))
        places.append(jnp.int32(n_cols))
        for pair in range(len(places) // 2):
            value = jnp.where(
                left, blocks[places[2 * pair], here, :], blocks[places[2 * pair + 1], here, :]
            )
            slots_ref[here, pair * 2 * BLOCK : (pair + 1) * 2 * BLOCK] = value.astype(BF16)


def diagonal_kernel(rows_ref, trans_ref, terms_ref):
    row, col, depth = (lax.axis_index(name) for name in ("row", "col", "depth"))
    part = rows_ref.shape[0]
    product = jnp.dot(rows_ref[...], trans_ref[...], preferred_element_type=F32)
    eye = lax.broadcasted_iota(jnp.int32, (part, part), 0) == lanes(part, part)
    share = jnp.sum(jnp.where(eye, product, 0.0), axis=0, keepdims=True)
    own = rows_ref[:, pl.ds(pl.multiple_of(depth * part, part), part)].astype(F32)
    own = jnp.where(row == col, 1.0, 0.0) * jnp.sum(jnp.where(eye, own, 0.0), axis=0, keepdims=True)
    rows8 = lax.broadcasted_iota(jnp.int32, (8, part), 0)
    full = jnp.where(rows8 < 6, jnp.broadcast_to(share, (8, part)), jnp.broadcast_to(own, (8, part)))
    base = jnp.where(rows8 % 2 == 0, pltpu.roll(full, BLOCK, 1), full)
    high = base.astype(BF16).astype(F32)
    middle = (base - high).astype(BF16).astype(F32)
    low = (base - high - middle).astype(BF16).astype(F32)
    terms_ref[...] = jnp.where(rows8 < 2, high, jnp.where(rows8 < 4, middle, jnp.where(rows8 < 6, low, base)))


def share_kernel(terms_ref, parts_ref, out_ref):
    total = parts_ref[0].astype(F32)
    for source in range(1, parts_ref.shape[0]):
        total = total + parts_ref[source].astype(F32)
    part = terms_ref.shape[1]
    wide = total.shape[1]
    last = jnp.where(lanes(8, part) < BLOCK, total[:, wide - part :], terms_ref[...])
    send = jnp.concatenate([total[:, : wide - part], last], axis=1).astype(BF16)
    for target in range(out_ref.shape[0]):
        out_ref[target] = send


def held_at(block_row, row, n_rows):
    owner = block_row // n_rows
    distance = (owner // 2 - row // 2) & 7
    place = (jnp.int32(PLACES) >> (distance * 4)) & 7
    place = place + ((owner ^ row) & 1) * 8
    return place * n_rows + block_row % n_rows


def from_chip(distance, value):
    n_row = lax.axis_size("row")
    return lax.ppermute(value, "row", [(s, (s - 2 * distance) % n_row) for s in range(n_row)])


def pair_kernel(own_ref, other_ref, pair_ref):
    rows = own_ref.shape[0]
    pair_ref[0:rows, :] = own_ref[...]
    pair_ref[rows : 2 * rows, :] = other_ref[...]


def gather_strip(strip, across):
    n_row = lax.axis_size("row")
    rows, width = strip.shape
    pair = pl.pallas_call(
        pair_kernel,
        out_shape=jax.ShapeDtypeStruct((2 * rows, width), strip.dtype),
        in_specs=[VMEM, VMEM],
        out_specs=VMEM,
        compiler_params=pltpu.CompilerParams(vmem_limit_bytes=24 << 20),
        cost_estimate=pl.CostEstimate(flops=PAIR_COST, bytes_accessed=1 << 19, transcendentals=0),
        name="pair",
    )(strip, across)
    above, below = from_chip(1, pair), from_chip(-1, pair)
    second, sixth = from_chip(2, strip), from_chip(-2, strip)
    held = jnp.concatenate([pair, second, sixth, above, below], axis=0)
    return held, lax.ppermute(held, "row", [(s, s ^ 1) for s in range(n_row)])


def plan_kernel(pat_ref, _, plan_ref):
    row, col, depth = (lax.axis_index(name) for name in ("row", "col", "depth"))
    n_rows, names = pat_ref.shape
    blocks = n_rows // lax.axis_size("depth")
    listed = pat_ref[...]
    own = row * n_rows + lax.broadcasted_iota(jnp.int32, (n_rows, 1), 0)
    bits = jnp.zeros((n_rows, 1), jnp.int32)
    for j in range(blocks):
        block = col * n_rows + depth * blocks + j
        hits = jnp.max(jnp.where(listed == block, 1, 0), axis=1, keepdims=True)
        bits = bits + jnp.where((hits == 1) | (own == block), 1 << j, 0)
    plan_ref[:, 0:names] = held_at(listed, row, n_rows) * BLOCK
    plan_ref[:, names : names + 1] = held_at(own, row, n_rows) * BLOCK
    plan_ref[:, names + 1 : names + 2] = bits


def product_kernel(
    plan_ref, flag_ref, count_ref, strip_ref, slots_ref, even_ref, odd_ref, out_ref, pop_ref, full
):
    n_rows, slots = plan_ref.shape[0], plan_ref.shape[1] - 1
    width = strip_ref.shape[1]
    which = lanes(BLOCK, width) // BLOCK
    half = even_ref.shape[0]
    full[0:half, :] = even_ref[...]
    full[half : 2 * half, :] = odd_ref[...]
    atoms = count_ref.shape[1]
    span = 2 * BLOCK
    wide = slots_ref.shape[1]
    low = lax.broadcasted_iota(jnp.int32, (atoms, atoms), 0)
    counts = jnp.broadcast_to(count_ref[...].astype(F32), (atoms, atoms))
    ends = jnp.sum(jnp.where(lanes(atoms, atoms) <= low, counts, 0.0), axis=1, keepdims=True)
    starts = jnp.sum(jnp.where(lanes(atoms, atoms) < low, counts, 0.0), axis=1, keepdims=True)
    at = lanes(atoms, span)
    total = jnp.zeros((atoms, span), F32)
    per_depth = 2 * BLOCK
    for d in range(n_rows // 2):
        terms = slots_ref[d * per_depth : (d + 1) * per_depth, wide - span :].astype(F32)
        terms = jnp.sum(terms.reshape(per_depth // 8, 8, span), axis=0)
        for u in range(2):
            squared = terms[u : u + 1] + terms[u + 2 : u + 3] + terms[u + 4 : u + 5]
            flag = jnp.broadcast_to(flag_ref[2 * d + u], squared.shape)
            diag = jnp.where(flag == 1, squared, 2.0 * terms[u + 6 : u + 7] - squared)
            diag = diag.astype(BF16).astype(F32)
            place = (at + ((2 * d + u) * BLOCK - BLOCK)).astype(F32)
            inside = (place >= starts) & (place < ends) & (at >= BLOCK)
            total = total + jnp.where(inside, jnp.broadcast_to(diag, (atoms, span)), 0.0)
    ones = jnp.ones((8, span), F32)
    sums = lax.dot_general(
        ones, total, (((1,), (1,)), ((), ())), precision=lax.Precision.HIGHEST, preferred_element_type=F32
    )
    pop_ref[...] = sums[0:1]
    for i in range(n_rows):
        here = pl.ds(i * BLOCK, BLOCK)
        squared = jnp.zeros((BLOCK, width), F32)
        for first in range(0, slots, GROUP):
            last = min(first + GROUP, slots)
            starts = [pl.multiple_of(plan_ref[i, slot], BLOCK) for slot in range(first, last)]
            chosen = jnp.concatenate([full[pl.ds(start, BLOCK), :] for start in starts], axis=0)
            values = slots_ref[here, first * BLOCK : last * BLOCK]
            squared = squared + jnp.dot(values, chosen, preferred_element_type=F32)
        keep = (plan_ref[i, slots] >> which) & 1
        own = strip_ref[here, :].astype(F32)
        flag = jnp.broadcast_to(flag_ref[i], squared.shape)
        value = jnp.where(flag == 1, squared, 2.0 * own - squared)
        out_ref[here, :] = jnp.where(keep == 1, value, 0.0).astype(BF16)


def per_device(density, pattern, orbital_counts, branch_flag):
    tile = density.shape[0]
    n_row, n_col, n_depth = (lax.axis_size(name) for name in ("row", "col", "depth"))
    width = tile // n_depth
    n_rows, names = pattern.shape
    slots_wide = (names + 2) * BLOCK
    limit = pltpu.CompilerParams(vmem_limit_bytes=24 << 20)
    strip, rows, slots = pl.pallas_call(
        pack_kernel,
        out_shape=(
            jax.ShapeDtypeStruct((tile, width), BF16),
            jax.ShapeDtypeStruct((width, tile), BF16),
            jax.ShapeDtypeStruct((width, slots_wide), BF16),
        ),
        in_specs=[HBM, HBM],
        out_specs=(VMEM, VMEM, VMEM),
        scratch_shapes=[
            pltpu.SMEM(pattern.shape, jnp.int32),
            pltpu.VMEM(density.shape, BF16),
            pltpu.VMEM((tile // BLOCK + 1, width, 2 * BLOCK), F32),
            pltpu.SemaphoreType.DMA((2,)),
        ],
        compiler_params=pltpu.CompilerParams(vmem_limit_bytes=60 << 20),
        name="pack",
    )(pattern, density)
    swap = [(r * n_col + c, c * n_col + r) for r in range(n_row) for c in range(n_col)]
    trans = lax.ppermute(strip, ("row", "col"), swap)
    chunk = width // n_col
    parts = lax.all_to_all(slots.reshape(n_col, chunk, slots_wide), "col", 0, 0)
    across = from_chip(4, strip)
    terms = pl.pallas_call(
        diagonal_kernel,
        out_shape=jax.ShapeDtypeStruct((8, width), F32),
        in_specs=[VMEM, VMEM],
        out_specs=VMEM,
        compiler_params=limit,
        cost_estimate=pl.CostEstimate(flops=COST, bytes_accessed=1 << 20, transcendentals=0),
        name="diagonal",
    )(rows, trans)
    send = pl.pallas_call(
        share_kernel,
        out_shape=jax.ShapeDtypeStruct((n_depth * n_col, chunk, slots_wide), BF16),
        in_specs=[VMEM, VMEM],
        out_specs=VMEM,
        compiler_params=limit,
        name="share",
    )(terms, parts)
    held, other = gather_strip(strip, across)
    stripe = lax.all_to_all(send, ("depth", "col"), 0, 0).reshape(tile, slots_wide)
    plan = pl.pallas_call(
        plan_kernel,
        out_shape=jax.ShapeDtypeStruct((n_rows, names + 2), jnp.int32),
        in_specs=[VMEM, pl.BlockSpec(memory_space=pl.ANY)],
        out_specs=VMEM,
        compiler_params=limit,
        cost_estimate=pl.CostEstimate(flops=1 << 31, bytes_accessed=1 << 12, transcendentals=0),
        name="plan",
    )(pattern, across)
    updated, populations = pl.pallas_call(
        product_kernel,
        out_shape=(
            jax.ShapeDtypeStruct((tile, width), BF16),
            jax.ShapeDtypeStruct((1, orbital_counts.shape[1]), F32),
        ),
        in_specs=[SMEM, SMEM, VMEM, VMEM, VMEM, VMEM, VMEM],
        out_specs=(VMEM, VMEM),
        scratch_shapes=[pltpu.VMEM((n_row * tile, width), BF16)],
        compiler_params=limit,
        name="product",
    )(plan, branch_flag, orbital_counts, strip, stripe, held, other)
    return (updated, populations.reshape(-1))


def solution(mesh):
    in_specs = (P("row", "col"), P("row", None), P("row", None), P("row"))
    out_specs = (P("row", ("col", "depth")), P("row"))
    return jax.shard_map(
        per_device, mesh=mesh, in_specs=in_specs, out_specs=out_specs, check_vma=False
    )
```

```python
import functools

import jax
import jax.numpy as jnp
from jax import lax
from jax.experimental import pallas as pl
from jax.experimental.pallas import tpu as pltpu
from jax.sharding import PartitionSpec as P

BLOCK = 64
VMEM = pl.BlockSpec(memory_space=pltpu.VMEM)
SMEM = pl.BlockSpec(memory_space=pltpu.SMEM)
HBM = pl.BlockSpec(memory_space=pltpu.HBM)
F32 = jnp.float32
BF16 = jnp.bfloat16
GROUP = 4
PLACES = 0x63517240
COST = int(5.3e9)
PAIR_COST = 1 << 33


def lanes(rows, count):
    return lax.broadcasted_iota(jnp.int32, (rows, count), 1)


def block_bits(pat_ref, block_row, own_block, first_col, count):
    bits = jnp.int32(0)
    for slot in range(pat_ref.shape[1] + 1):
        listed = own_block if slot == pat_ref.shape[1] else pat_ref[block_row, slot]
        local = listed - first_col
        inside = (local >= 0) & (local < count)
        bits = bits | jnp.where(inside, jnp.int32(1) << jnp.clip(local, 0, count - 1), 0)
    return bits


def pack_kernel(pat_hbm, dens_hbm, strip_ref, rows_ref, slots_ref, pat_ref, dens_ref, blocks, done):
    pat_copy = pltpu.make_async_copy(pat_hbm, pat_ref, done.at[0])
    dens_copy = pltpu.make_async_copy(dens_hbm, dens_ref, done.at[1])
    pat_copy.start()
    dens_copy.start()
    row, col, depth = (lax.axis_index(name) for name in ("row", "col", "depth"))
    n_rows, names = pat_ref.shape
    tile = dens_ref.shape[1]
    n_cols = tile // BLOCK
    width = strip_ref.shape[1]
    part = rows_ref.shape[0]
    first_col = col * n_cols
    start = pl.multiple_of(depth * width, width)
    which = lanes(BLOCK, width) // BLOCK
    pat_copy.wait()
    kept = [block_bits(pat_ref, i, row * n_rows + i, first_col, n_cols) for i in range(n_rows)]
    dens_copy.wait()
    for i, bits in enumerate(kept):
        keep = (lax.shift_right_logical(bits, depth * (width // BLOCK)) >> which) & 1
        here = pl.ds(i * BLOCK, BLOCK)
        value = dens_ref[here, pl.ds(start, width)].astype(F32)
        strip_ref[here, :] = jnp.where(keep == 1, value, 0.0).astype(BF16)
    first_row = depth * (part // BLOCK)
    begin = pl.multiple_of(depth * part, part)
    which = lanes(BLOCK, tile) // BLOCK
    blocks[n_cols] = jnp.zeros_like(blocks[n_cols])
    for u in range(part // BLOCK):
        i = first_row + u
        bits = block_bits(pat_ref, i, row * n_rows + i, first_col, n_cols)
        value = dens_ref[pl.ds(pl.multiple_of(begin + u * BLOCK, BLOCK), BLOCK), :].astype(F32)
        value = jnp.where(((bits >> which) & 1) == 1, value, 0.0)
        here = pl.ds(u * BLOCK, BLOCK)
        rows_ref[here, :] = value.astype(BF16)
        for j in range(n_cols):
            one = value[:, j * BLOCK : (j + 1) * BLOCK]
            blocks[j, here, :] = jnp.concatenate([one, one], axis=1)
    left = lanes(BLOCK, 2 * BLOCK) < BLOCK
    for u in range(part // BLOCK):
        i = first_row + u
        own_block = row * n_rows + i
        here = pl.ds(u * BLOCK, BLOCK)
        places = []
        repeated = jnp.int32(0)
        for slot in range(names):
            listed = pat_ref[i, slot]
            local = listed - first_col
            places.append(jnp.where((local >= 0) & (local < n_cols), local, n_cols))
            repeated = repeated | jnp.where(listed == own_block, 1, 0)
        local = own_block - first_col
        inside = (local >= 0) & (local < n_cols) & (repeated == 0)
        places.append(jnp.where(inside, local, n_cols))
        places.append(jnp.int32(n_cols))
        for pair in range(len(places) // 2):
            value = jnp.where(
                left, blocks[places[2 * pair], here, :], blocks[places[2 * pair + 1], here, :]
            )
            slots_ref[here, pair * 2 * BLOCK : (pair + 1) * 2 * BLOCK] = value.astype(BF16)


def diagonal_kernel(rows_ref, trans_ref, terms_ref):
    row, col, depth = (lax.axis_index(name) for name in ("row", "col", "depth"))
    part = rows_ref.shape[0]
    product = jnp.dot(rows_ref[...], trans_ref[...], preferred_element_type=F32)
    eye = lax.broadcasted_iota(jnp.int32, (part, part), 0) == lanes(part, part)
    share = jnp.sum(jnp.where(eye, product, 0.0), axis=0, keepdims=True)
    own = rows_ref[:, pl.ds(pl.multiple_of(depth * part, part), part)].astype(F32)
    own = jnp.where(row == col, 1.0, 0.0) * jnp.sum(jnp.where(eye, own, 0.0), axis=0, keepdims=True)
    rows8 = lax.broadcasted_iota(jnp.int32, (8, part), 0)
    full = jnp.where(rows8 < 6, jnp.broadcast_to(share, (8, part)), jnp.broadcast_to(own, (8, part)))
    base = jnp.where(rows8 % 2 == 0, pltpu.roll(full, BLOCK, 1), full)
    high = base.astype(BF16).astype(F32)
    middle = (base - high).astype(BF16).astype(F32)
    low = (base - high - middle).astype(BF16).astype(F32)
    terms_ref[...] = jnp.where(rows8 < 2, high, jnp.where(rows8 < 4, middle, jnp.where(rows8 < 6, low, base)))


def share_kernel(terms_ref, parts_ref, out_ref):
    total = parts_ref[0].astype(F32)
    for source in range(1, parts_ref.shape[0]):
        total = total + parts_ref[source].astype(F32)
    part = terms_ref.shape[1]
    wide = total.shape[1]
    last = jnp.where(lanes(8, part) < BLOCK, total[:, wide - part :], terms_ref[...])
    send = jnp.concatenate([total[:, : wide - part], last], axis=1).astype(BF16)
    for target in range(out_ref.shape[0]):
        out_ref[target] = send


def held_at(block_row, row, n_rows):
    owner = block_row // n_rows
    distance = (owner // 2 - row // 2) & 7
    place = (jnp.int32(PLACES) >> (distance * 4)) & 7
    place = place + ((owner ^ row) & 1) * 8
    return place * n_rows + block_row % n_rows


def from_chip(distance, value):
    n_row = lax.axis_size("row")
    return lax.ppermute(value, "row", [(s, (s - 2 * distance) % n_row) for s in range(n_row)])


def pair_kernel(own_ref, other_ref, pair_ref):
    rows = own_ref.shape[0]
    pair_ref[0:rows, :] = own_ref[...]
    pair_ref[rows : 2 * rows, :] = other_ref[...]


def gather_strip(strip, across):
    n_row = lax.axis_size("row")
    rows, width = strip.shape
    pair = pl.pallas_call(
        pair_kernel,
        out_shape=jax.ShapeDtypeStruct((2 * rows, width), strip.dtype),
        in_specs=[VMEM, VMEM],
        out_specs=VMEM,
        compiler_params=pltpu.CompilerParams(vmem_limit_bytes=24 << 20),
        cost_estimate=pl.CostEstimate(flops=PAIR_COST, bytes_accessed=1 << 19, transcendentals=0),
        name="pair",
    )(strip, across)
    strip, pair = lax.optimization_barrier((strip, pair))
    above, below = from_chip(1, pair), from_chip(-1, pair)
    second, sixth = from_chip(2, strip), from_chip(-2, strip)
    held = jnp.concatenate([pair, second, sixth, above, below], axis=0)
    return held, lax.ppermute(held, "row", [(s, s ^ 1) for s in range(n_row)])


def plan_kernel(pat_ref, _, plan_ref):
    row, col, depth = (lax.axis_index(name) for name in ("row", "col", "depth"))
    n_rows, names = pat_ref.shape
    blocks = n_rows // lax.axis_size("depth")
    listed = pat_ref[...]
    own = row * n_rows + lax.broadcasted_iota(jnp.int32, (n_rows, 1), 0)
    bits = jnp.zeros((n_rows, 1), jnp.int32)
    for j in range(blocks):
        block = col * n_rows + depth * blocks + j
        hits = jnp.max(jnp.where(listed == block, 1, 0), axis=1, keepdims=True)
        bits = bits + jnp.where((hits == 1) | (own == block), 1 << j, 0)
    plan_ref[:, 0:names] = held_at(listed, row, n_rows) * BLOCK
    plan_ref[:, names : names + 1] = held_at(own, row, n_rows) * BLOCK
    plan_ref[:, names + 1 : names + 2] = bits


def product_kernel(
    plan_ref, flag_ref, count_ref, strip_ref, slots_ref, even_ref, odd_ref, out_ref, pop_ref, full
):
    n_rows, slots = plan_ref.shape[0], plan_ref.shape[1] - 1
    width = strip_ref.shape[1]
    which = lanes(BLOCK, width) // BLOCK
    half = even_ref.shape[0]
    full[0:half, :] = even_ref[...]
    full[half : 2 * half, :] = odd_ref[...]
    atoms = count_ref.shape[1]
    span = 2 * BLOCK
    wide = slots_ref.shape[1]
    low = lax.broadcasted_iota(jnp.int32, (atoms, atoms), 0)
    counts = jnp.broadcast_to(count_ref[...].astype(F32), (atoms, atoms))
    ends = jnp.sum(jnp.where(lanes(atoms, atoms) <= low, counts, 0.0), axis=1, keepdims=True)
    starts = jnp.sum(jnp.where(lanes(atoms, atoms) < low, counts, 0.0), axis=1, keepdims=True)
    at = lanes(atoms, span)
    total = jnp.zeros((atoms, span), F32)
    per_depth = 2 * BLOCK
    for d in range(n_rows // 2):
        terms = slots_ref[d * per_depth : (d + 1) * per_depth, wide - span :].astype(F32)
        terms = jnp.sum(terms.reshape(per_depth // 8, 8, span), axis=0)
        for u in range(2):
            squared = terms[u : u + 1] + terms[u + 2 : u + 3] + terms[u + 4 : u + 5]
            flag = jnp.broadcast_to(flag_ref[2 * d + u], squared.shape)
            diag = jnp.where(flag == 1, squared, 2.0 * terms[u + 6 : u + 7] - squared)
            diag = diag.astype(BF16).astype(F32)
            place = (at + ((2 * d + u) * BLOCK - BLOCK)).astype(F32)
            inside = (place >= starts) & (place < ends) & (at >= BLOCK)
            total = total + jnp.where(inside, jnp.broadcast_to(diag, (atoms, span)), 0.0)
    ones = jnp.ones((8, span), F32)
    sums = lax.dot_general(
        ones, total, (((1,), (1,)), ((), ())), precision=lax.Precision.HIGHEST, preferred_element_type=F32
    )
    pop_ref[...] = sums[0:1]
    for i in range(n_rows):
        here = pl.ds(i * BLOCK, BLOCK)
        squared = jnp.zeros((BLOCK, width), F32)
        for first in range(0, slots, GROUP):
            last = min(first + GROUP, slots)
            starts = [pl.multiple_of(plan_ref[i, slot], BLOCK) for slot in range(first, last)]
            chosen = jnp.concatenate([full[pl.ds(start, BLOCK), :] for start in starts], axis=0)
            values = slots_ref[here, first * BLOCK : last * BLOCK]
            squared = squared + jnp.dot(values, chosen, preferred_element_type=F32)
        keep = (plan_ref[i, slots] >> which) & 1
        own = strip_ref[here, :].astype(F32)
        flag = jnp.broadcast_to(flag_ref[i], squared.shape)
        value = jnp.where(flag == 1, squared, 2.0 * own - squared)
        out_ref[here, :] = jnp.where(keep == 1, value, 0.0).astype(BF16)


def per_device(density, pattern, orbital_counts, branch_flag):
    tile = density.shape[0]
    n_row, n_col, n_depth = (lax.axis_size(name) for name in ("row", "col", "depth"))
    width = tile // n_depth
    n_rows, names = pattern.shape
    slots_wide = (names + 2) * BLOCK
    limit = pltpu.CompilerParams(vmem_limit_bytes=24 << 20)
    strip, rows, slots = pl.pallas_call(
        pack_kernel,
        out_shape=(
            jax.ShapeDtypeStruct((tile, width), BF16),
            jax.ShapeDtypeStruct((width, tile), BF16),
            jax.ShapeDtypeStruct((width, slots_wide), BF16),
        ),
        in_specs=[HBM, HBM],
        out_specs=(VMEM, VMEM, VMEM),
        scratch_shapes=[
            pltpu.SMEM(pattern.shape, jnp.int32),
            pltpu.VMEM(density.shape, BF16),
            pltpu.VMEM((tile // BLOCK + 1, width, 2 * BLOCK), F32),
            pltpu.SemaphoreType.DMA((2,)),
        ],
        compiler_params=pltpu.CompilerParams(vmem_limit_bytes=60 << 20),
        name="pack",
    )(pattern, density)
    swap = [(r * n_col + c, c * n_col + r) for r in range(n_row) for c in range(n_col)]
    trans = lax.ppermute(strip, ("row", "col"), swap)
    chunk = width // n_col
    parts = lax.all_to_all(slots.reshape(n_col, chunk, slots_wide), "col", 0, 0)
    across = from_chip(4, strip)
    terms = pl.pallas_call(
        diagonal_kernel,
        out_shape=jax.ShapeDtypeStruct((8, width), F32),
        in_specs=[VMEM, VMEM],
        out_specs=VMEM,
        compiler_params=pltpu.CompilerParams(vmem_limit_bytes=60 << 20),
        cost_estimate=pl.CostEstimate(flops=COST, bytes_accessed=1 << 20, transcendentals=0),
        name="diagonal",
    )(rows, trans)
    send = pl.pallas_call(
        share_kernel,
        out_shape=jax.ShapeDtypeStruct((n_depth * n_col, chunk, slots_wide), BF16),
        in_specs=[VMEM, VMEM],
        out_specs=VMEM,
        compiler_params=limit,
        name="share",
    )(terms, parts)
    held, other = gather_strip(strip, across)
    stripe = lax.all_to_all(send, ("depth", "col"), 0, 0).reshape(tile, slots_wide)
    plan = pl.pallas_call(
        plan_kernel,
        out_shape=jax.ShapeDtypeStruct((n_rows, names + 2), jnp.int32),
        in_specs=[VMEM, pl.BlockSpec(memory_space=pl.ANY)],
        out_specs=VMEM,
        compiler_params=limit,
        cost_estimate=pl.CostEstimate(flops=1 << 31, bytes_accessed=1 << 12, transcendentals=0),
        name="plan",
    )(pattern, across)
    updated, populations = pl.pallas_call(
        product_kernel,
        out_shape=(
            jax.ShapeDtypeStruct((tile, width), BF16),
            jax.ShapeDtypeStruct((1, orbital_counts.shape[1]), F32),
        ),
        in_specs=[SMEM, SMEM, VMEM, VMEM, VMEM, VMEM, VMEM],
        out_specs=(VMEM, VMEM),
        scratch_shapes=[pltpu.VMEM((n_row * tile, width), BF16)],
        compiler_params=limit,
        name="product",
    )(plan, branch_flag, orbital_counts, strip, stripe, held, other)
    return (updated, populations.reshape(-1))


def solution(mesh):
    in_specs = (P("row", "col"), P("row", None), P("row", None), P("row"))
    out_specs = (P("row", ("col", "depth")), P("row"))
    return jax.shard_map(
        per_device, mesh=mesh, in_specs=in_specs, out_specs=out_specs, check_vma=False
    )
```

```python
import functools

import jax
import jax.numpy as jnp
from jax import lax
from jax.experimental import pallas as pl
from jax.experimental.pallas import tpu as pltpu
from jax.sharding import PartitionSpec as P

BLOCK = 64
VMEM = pl.BlockSpec(memory_space=pltpu.VMEM)
SMEM = pl.BlockSpec(memory_space=pltpu.SMEM)
HBM = pl.BlockSpec(memory_space=pltpu.HBM)
F32 = jnp.float32
BF16 = jnp.bfloat16
GROUP = 4
PLACES = 0x63517240
COST = int(5.3e9)
PAIR_COST = 1 << 33


def lanes(rows, count):
    return lax.broadcasted_iota(jnp.int32, (rows, count), 1)


def block_bits(pat_ref, block_row, own_block, first_col, count):
    bits = jnp.int32(0)
    for slot in range(pat_ref.shape[1] + 1):
        listed = own_block if slot == pat_ref.shape[1] else pat_ref[block_row, slot]
        local = listed - first_col
        inside = (local >= 0) & (local < count)
        bits = bits | jnp.where(inside, jnp.int32(1) << jnp.clip(local, 0, count - 1), 0)
    return bits


def pack_kernel(pat_hbm, dens_hbm, strip_ref, rows_ref, slots_ref, pat_ref, dens_ref, blocks, done):
    pat_copy = pltpu.make_async_copy(pat_hbm, pat_ref, done.at[0])
    dens_copy = pltpu.make_async_copy(dens_hbm, dens_ref, done.at[1])
    pat_copy.start()
    dens_copy.start()
    row, col, depth = (lax.axis_index(name) for name in ("row", "col", "depth"))
    n_rows, names = pat_ref.shape
    tile = dens_ref.shape[1]
    n_cols = tile // BLOCK
    width = strip_ref.shape[1]
    part = rows_ref.shape[0]
    first_col = col * n_cols
    start = pl.multiple_of(depth * width, width)
    which = lanes(BLOCK, width) // BLOCK
    pat_copy.wait()
    kept = [block_bits(pat_ref, i, row * n_rows + i, first_col, n_cols) for i in range(n_rows)]
    dens_copy.wait()
    for i, bits in enumerate(kept):
        keep = (lax.shift_right_logical(bits, depth * (width // BLOCK)) >> which) & 1
        here = pl.ds(i * BLOCK, BLOCK)
        value = dens_ref[here, pl.ds(start, width)].astype(F32)
        strip_ref[here, :] = jnp.where(keep == 1, value, 0.0).astype(BF16)
    first_row = depth * (part // BLOCK)
    begin = pl.multiple_of(depth * part, part)
    which = lanes(BLOCK, tile) // BLOCK
    blocks[n_cols] = jnp.zeros_like(blocks[n_cols])
    for u in range(part // BLOCK):
        i = first_row + u
        bits = block_bits(pat_ref, i, row * n_rows + i, first_col, n_cols)
        value = dens_ref[pl.ds(pl.multiple_of(begin + u * BLOCK, BLOCK), BLOCK), :].astype(F32)
        value = jnp.where(((bits >> which) & 1) == 1, value, 0.0)
        here = pl.ds(u * BLOCK, BLOCK)
        rows_ref[here, :] = value.astype(BF16)
        for j in range(n_cols):
            one = value[:, j * BLOCK : (j + 1) * BLOCK]
            blocks[j, here, :] = jnp.concatenate([one, one], axis=1)
    left = lanes(BLOCK, 2 * BLOCK) < BLOCK
    for u in range(part // BLOCK):
        i = first_row + u
        own_block = row * n_rows + i
        here = pl.ds(u * BLOCK, BLOCK)
        places = []
        repeated = jnp.int32(0)
        for slot in range(names):
            listed = pat_ref[i, slot]
            local = listed - first_col
            places.append(jnp.where((local >= 0) & (local < n_cols), local, n_cols))
            repeated = repeated | jnp.where(listed == own_block, 1, 0)
        local = own_block - first_col
        inside = (local >= 0) & (local < n_cols) & (repeated == 0)
        places.append(jnp.where(inside, local, n_cols))
        places.append(jnp.int32(n_cols))
        for pair in range(len(places) // 2):
            value = jnp.where(
                left, blocks[places[2 * pair], here, :], blocks[places[2 * pair + 1], here, :]
            )
            slots_ref[here, pair * 2 * BLOCK : (pair + 1) * 2 * BLOCK] = value.astype(BF16)


def diagonal_kernel(rows_ref, trans_ref, terms_ref):
    row, col, depth = (lax.axis_index(name) for name in ("row", "col", "depth"))
    part = rows_ref.shape[0]
    product = jnp.dot(rows_ref[...], trans_ref[...], preferred_element_type=F32)
    eye = lax.broadcasted_iota(jnp.int32, (part, part), 0) == lanes(part, part)
    share = jnp.sum(jnp.where(eye, product, 0.0), axis=0, keepdims=True)
    own = rows_ref[:, pl.ds(pl.multiple_of(depth * part, part), part)].astype(F32)
    own = jnp.where(row == col, 1.0, 0.0) * jnp.sum(jnp.where(eye, own, 0.0), axis=0, keepdims=True)
    rows8 = lax.broadcasted_iota(jnp.int32, (8, part), 0)
    full = jnp.where(rows8 < 6, jnp.broadcast_to(share, (8, part)), jnp.broadcast_to(own, (8, part)))
    base = jnp.where(rows8 % 2 == 0, pltpu.roll(full, BLOCK, 1), full)
    high = base.astype(BF16).astype(F32)
    middle = (base - high).astype(BF16).astype(F32)
    low = (base - high - middle).astype(BF16).astype(F32)
    terms_ref[...] = jnp.where(rows8 < 2, high, jnp.where(rows8 < 4, middle, jnp.where(rows8 < 6, low, base)))


def share_kernel(terms_ref, parts_ref, out_ref):
    total = parts_ref[0].astype(F32)
    for source in range(1, parts_ref.shape[0]):
        total = total + parts_ref[source].astype(F32)
    part = terms_ref.shape[1]
    wide = total.shape[1]
    last = jnp.where(lanes(8, part) < BLOCK, total[:, wide - part :], terms_ref[...])
    send = jnp.concatenate([total[:, : wide - part], last], axis=1).astype(BF16)
    for target in range(out_ref.shape[0]):
        out_ref[target] = send


def held_at(block_row, row, n_rows):
    owner = block_row // n_rows
    distance = (owner // 2 - row // 2) & 7
    place = (jnp.int32(PLACES) >> (distance * 4)) & 7
    place = place + ((owner ^ row) & 1) * 8
    return place * n_rows + block_row % n_rows


def from_chip(distance, value):
    n_row = lax.axis_size("row")
    return lax.ppermute(value, "row", [(s, (s - 2 * distance) % n_row) for s in range(n_row)])


def pair_kernel(own_ref, other_ref, pair_ref):
    rows = own_ref.shape[0]
    pair_ref[0:rows, :] = own_ref[...]
    pair_ref[rows : 2 * rows, :] = other_ref[...]


def gather_strip(strip, across):
    n_row = lax.axis_size("row")
    rows, width = strip.shape
    pair = pl.pallas_call(
        pair_kernel,
        out_shape=jax.ShapeDtypeStruct((2 * rows, width), strip.dtype),
        in_specs=[VMEM, VMEM],
        out_specs=VMEM,
        compiler_params=pltpu.CompilerParams(vmem_limit_bytes=24 << 20),
        cost_estimate=pl.CostEstimate(flops=PAIR_COST, bytes_accessed=1 << 19, transcendentals=0),
        name="pair",
    )(strip, across)
    strip, pair = lax.optimization_barrier((strip, pair))
    above, below = from_chip(1, pair), from_chip(-1, pair)
    second, sixth = from_chip(2, strip), from_chip(-2, strip)
    held = jnp.concatenate([pair, second, sixth, above, below], axis=0)
    return held, lax.ppermute(held, "row", [(s, s ^ 1) for s in range(n_row)])


def plan_kernel(pat_ref, _, plan_ref):
    row, col, depth = (lax.axis_index(name) for name in ("row", "col", "depth"))
    n_rows, names = pat_ref.shape
    blocks = n_rows // lax.axis_size("depth")
    listed = pat_ref[...]
    own = row * n_rows + lax.broadcasted_iota(jnp.int32, (n_rows, 1), 0)
    bits = jnp.zeros((n_rows, 1), jnp.int32)
    for j in range(blocks):
        block = col * n_rows + depth * blocks + j
        hits = jnp.max(jnp.where(listed == block, 1, 0), axis=1, keepdims=True)
        bits = bits + jnp.where((hits == 1) | (own == block), 1 << j, 0)
    plan_ref[:, 0:names] = held_at(listed, row, n_rows) * BLOCK
    plan_ref[:, names : names + 1] = held_at(own, row, n_rows) * BLOCK
    plan_ref[:, names + 1 : names + 2] = bits


def product_kernel(
    plan_ref, flag_ref, count_ref, strip_ref, slots_ref, even_ref, odd_ref, out_ref, pop_ref, full
):
    n_rows, slots = plan_ref.shape[0], plan_ref.shape[1] - 1
    width = strip_ref.shape[1]
    which = lanes(BLOCK, width) // BLOCK
    half = even_ref.shape[0]
    full[0:half, :] = even_ref[...]
    full[half : 2 * half, :] = odd_ref[...]
    atoms = count_ref.shape[1]
    span = 2 * BLOCK
    wide = slots_ref.shape[1]
    low = lax.broadcasted_iota(jnp.int32, (atoms, atoms), 0)
    counts = jnp.broadcast_to(count_ref[...].astype(F32), (atoms, atoms))
    ends = jnp.sum(jnp.where(lanes(atoms, atoms) <= low, counts, 0.0), axis=1, keepdims=True)
    starts = jnp.sum(jnp.where(lanes(atoms, atoms) < low, counts, 0.0), axis=1, keepdims=True)
    at = lanes(atoms, span)
    total = jnp.zeros((atoms, span), F32)
    per_depth = 2 * BLOCK
    for d in range(n_rows // 2):
        terms = slots_ref[d * per_depth : (d + 1) * per_depth, wide - span :].astype(F32)
        terms = jnp.sum(terms.reshape(per_depth // 8, 8, span), axis=0)
        for u in range(2):
            squared = terms[u : u + 1] + terms[u + 2 : u + 3] + terms[u + 4 : u + 5]
            flag = jnp.broadcast_to(flag_ref[2 * d + u], squared.shape)
            diag = jnp.where(flag == 1, squared, 2.0 * terms[u + 6 : u + 7] - squared)
            diag = diag.astype(BF16).astype(F32)
            place = (at + ((2 * d + u) * BLOCK - BLOCK)).astype(F32)
            inside = (place >= starts) & (place < ends) & (at >= BLOCK)
            total = total + jnp.where(inside, jnp.broadcast_to(diag, (atoms, span)), 0.0)
    ones = jnp.ones((8, span), F32)
    sums = lax.dot_general(
        ones, total, (((1,), (1,)), ((), ())), precision=lax.Precision.HIGHEST, preferred_element_type=F32
    )
    pop_ref[...] = sums[0:1]
    for i in range(n_rows):
        here = pl.ds(i * BLOCK, BLOCK)
        squared = jnp.zeros((BLOCK, width), F32)
        for first in range(0, slots, GROUP):
            last = min(first + GROUP, slots)
            starts = [pl.multiple_of(plan_ref[i, slot], BLOCK) for slot in range(first, last)]
            chosen = jnp.concatenate([full[pl.ds(start, BLOCK), :] for start in starts], axis=0)
            values = slots_ref[here, first * BLOCK : last * BLOCK]
            squared = squared + jnp.dot(values, chosen, preferred_element_type=F32)
        keep = (plan_ref[i, slots] >> which) & 1
        own = strip_ref[here, :].astype(F32)
        flag = jnp.broadcast_to(flag_ref[i], squared.shape)
        value = jnp.where(flag == 1, squared, 2.0 * own - squared)
        out_ref[here, :] = jnp.where(keep == 1, value, 0.0).astype(BF16)


def per_device(density, pattern, orbital_counts, branch_flag):
    tile = density.shape[0]
    n_row, n_col, n_depth = (lax.axis_size(name) for name in ("row", "col", "depth"))
    width = tile // n_depth
    n_rows, names = pattern.shape
    slots_wide = (names + 2) * BLOCK
    limit = pltpu.CompilerParams(vmem_limit_bytes=24 << 20)
    strip, rows, slots = pl.pallas_call(
        pack_kernel,
        out_shape=(
            jax.ShapeDtypeStruct((tile, width), BF16),
            jax.ShapeDtypeStruct((width, tile), BF16),
            jax.ShapeDtypeStruct((width, slots_wide), BF16),
        ),
        in_specs=[HBM, HBM],
        out_specs=(VMEM, VMEM, VMEM),
        scratch_shapes=[
            pltpu.SMEM(pattern.shape, jnp.int32),
            pltpu.VMEM(density.shape, BF16),
            pltpu.VMEM((tile // BLOCK + 1, width, 2 * BLOCK), F32),
            pltpu.SemaphoreType.DMA((2,)),
        ],
        compiler_params=pltpu.CompilerParams(vmem_limit_bytes=60 << 20),
        name="pack",
    )(pattern, density)
    swap = [(r * n_col + c, c * n_col + r) for r in range(n_row) for c in range(n_col)]
    trans = lax.ppermute(strip, ("row", "col"), swap)
    chunk = width // n_col
    parts = lax.all_to_all(slots.reshape(n_col, chunk, slots_wide), "col", 0, 0)
    across = from_chip(4, strip)
    terms = pl.pallas_call(
        diagonal_kernel,
        out_shape=jax.ShapeDtypeStruct((8, width), F32),
        in_specs=[VMEM, VMEM],
        out_specs=VMEM,
        compiler_params=limit,
        cost_estimate=pl.CostEstimate(flops=COST, bytes_accessed=1 << 20, transcendentals=0),
        name="diagonal",
    )(rows, trans)
    send = pl.pallas_call(
        share_kernel,
        out_shape=jax.ShapeDtypeStruct((n_depth * n_col, chunk, slots_wide), BF16),
        in_specs=[VMEM, VMEM],
        out_specs=VMEM,
        compiler_params=limit,
        name="share",
    )(terms, parts)
    held, other = gather_strip(strip, across)
    stripe = lax.all_to_all(send, ("depth", "col"), 0, 0).reshape(tile, slots_wide)
    plan = pl.pallas_call(
        plan_kernel,
        out_shape=jax.ShapeDtypeStruct((n_rows, names + 2), jnp.int32),
        in_specs=[VMEM, pl.BlockSpec(memory_space=pl.ANY)],
        out_specs=VMEM,
        compiler_params=limit,
        cost_estimate=pl.CostEstimate(flops=1 << 31, bytes_accessed=1 << 12, transcendentals=0),
        name="plan",
    )(pattern, across)
    updated, populations = pl.pallas_call(
        product_kernel,
        out_shape=(
            jax.ShapeDtypeStruct((tile, width), BF16),
            jax.ShapeDtypeStruct((1, orbital_counts.shape[1]), F32),
        ),
        in_specs=[SMEM, SMEM, VMEM, VMEM, VMEM, VMEM, VMEM],
        out_specs=(VMEM, VMEM),
        scratch_shapes=[pltpu.VMEM((n_row * tile, width), BF16)],
        compiler_params=limit,
        name="product",
    )(plan, branch_flag, orbital_counts, strip, stripe, held, other)
    return (updated, populations.reshape(-1))


def solution(mesh):
    in_specs = (P("row", "col"), P("row", None), P("row", None), P("row"))
    out_specs = (P("row", ("col", "depth")), P("row"))
    return jax.shard_map(
        per_device, mesh=mesh, in_specs=in_specs, out_specs=out_specs, check_vma=False
    )
```

```python
import functools

import jax
import jax.numpy as jnp
from jax import lax
from jax.experimental import pallas as pl
from jax.experimental.pallas import tpu as pltpu
from jax.sharding import PartitionSpec as P

BLOCK = 64
VMEM = pl.BlockSpec(memory_space=pltpu.VMEM)
SMEM = pl.BlockSpec(memory_space=pltpu.SMEM)
HBM = pl.BlockSpec(memory_space=pltpu.HBM)
F32 = jnp.float32
BF16 = jnp.bfloat16
GROUP = 4
PLACES = 0x63517240
COST = int(5.3e9)
PAIR_COST = 1 << 33


def lanes(rows, count):
    return lax.broadcasted_iota(jnp.int32, (rows, count), 1)


def block_bits(pat_ref, block_row, own_block, first_col, count):
    bits = jnp.int32(0)
    for slot in range(pat_ref.shape[1] + 1):
        listed = own_block if slot == pat_ref.shape[1] else pat_ref[block_row, slot]
        local = listed - first_col
        inside = (local >= 0) & (local < count)
        bits = bits | jnp.where(inside, jnp.int32(1) << jnp.clip(local, 0, count - 1), 0)
    return bits


def pack_kernel(pat_hbm, dens_hbm, strip_ref, rows_ref, slots_ref, pat_ref, pat_vec, dens_ref, blocks, done):
    pat_copy = pltpu.make_async_copy(pat_hbm, pat_ref, done.at[0])
    dens_copy = pltpu.make_async_copy(dens_hbm, dens_ref, done.at[1])
    vec_copy = pltpu.make_async_copy(pat_hbm, pat_vec, done.at[2])
    pat_copy.start()
    vec_copy.start()
    dens_copy.start()
    row, col, depth = (lax.axis_index(name) for name in ("row", "col", "depth"))
    n_rows, names = pat_ref.shape
    tile = dens_ref.shape[1]
    n_cols = tile // BLOCK
    width = strip_ref.shape[1]
    part = rows_ref.shape[0]
    first_col = col * n_cols
    start = pl.multiple_of(depth * width, width)
    which = lanes(BLOCK, width) // BLOCK
    vec_copy.wait()
    own = row * n_rows + lax.broadcasted_iota(jnp.int32, (n_rows, 1), 0)
    kept = jnp.zeros((n_rows, 1), jnp.int32)
    for j in range(width // BLOCK):
        block = first_col + depth * (width // BLOCK) + j
        hits = jnp.max(jnp.where(pat_vec[...] == block, 1, 0), axis=1, keepdims=True)
        kept = kept + jnp.where((hits == 1) | (own == block), 1 << j, 0)
    pat_copy.wait()
    first_row = depth * (part // BLOCK)
    row_bits, row_places = [], []
    for u in range(part // BLOCK):
        i = first_row + u
        own_block = row * n_rows + i
        row_bits.append(block_bits(pat_ref, i, own_block, first_col, n_cols))
        places = []
        repeated = jnp.int32(0)
        for slot in range(names):
            listed = pat_ref[i, slot]
            local = listed - first_col
            places.append(jnp.where((local >= 0) & (local < n_cols), local, n_cols))
            repeated = repeated | jnp.where(listed == own_block, 1, 0)
        local = own_block - first_col
        inside = (local >= 0) & (local < n_cols) & (repeated == 0)
        places.append(jnp.where(inside, local, n_cols))
        places.append(jnp.int32(n_cols))
        row_places.append(places)
    dens_copy.wait()
    for i in range(n_rows):
        keep = (jnp.broadcast_to(kept[i : i + 1, :], (BLOCK, width)) >> which) & 1
        here = pl.ds(i * BLOCK, BLOCK)
        value = dens_ref[here, pl.ds(start, width)].astype(F32)
        strip_ref[here, :] = jnp.where(keep == 1, value, 0.0).astype(BF16)
    begin = pl.multiple_of(depth * part, part)
    which = lanes(BLOCK, tile) // BLOCK
    blocks[n_cols] = jnp.zeros_like(blocks[n_cols])
    for u in range(part // BLOCK):
        bits = row_bits[u]
        value = dens_ref[pl.ds(pl.multiple_of(begin + u * BLOCK, BLOCK), BLOCK), :].astype(F32)
        value = jnp.where(((bits >> which) & 1) == 1, value, 0.0)
        here = pl.ds(u * BLOCK, BLOCK)
        rows_ref[here, :] = value.astype(BF16)
        for j in range(n_cols):
            one = value[:, j * BLOCK : (j + 1) * BLOCK]
            blocks[j, here, :] = jnp.concatenate([one, one], axis=1)
    left = lanes(BLOCK, 2 * BLOCK) < BLOCK
    for u, places in enumerate(row_places):
        here = pl.ds(u * BLOCK, BLOCK)
        for pair in range(len(places) // 2):
            value = jnp.where(
                left, blocks[places[2 * pair], here, :], blocks[places[2 * pair + 1], here, :]
            )
            slots_ref[here, pair * 2 * BLOCK : (pair + 1) * 2 * BLOCK] = value.astype(BF16)


def diagonal_kernel(rows_ref, trans_ref, terms_ref):
    row, col, depth = (lax.axis_index(name) for name in ("row", "col", "depth"))
    part = rows_ref.shape[0]
    product = jnp.dot(rows_ref[...], trans_ref[...], preferred_element_type=F32)
    eye = lax.broadcasted_iota(jnp.int32, (part, part), 0) == lanes(part, part)
    share = jnp.sum(jnp.where(eye, product, 0.0), axis=0, keepdims=True)
    own = rows_ref[:, pl.ds(pl.multiple_of(depth * part, part), part)].astype(F32)
    own = jnp.where(row == col, 1.0, 0.0) * jnp.sum(jnp.where(eye, own, 0.0), axis=0, keepdims=True)
    rows8 = lax.broadcasted_iota(jnp.int32, (8, part), 0)
    full = jnp.where(rows8 < 6, jnp.broadcast_to(share, (8, part)), jnp.broadcast_to(own, (8, part)))
    base = jnp.where(rows8 % 2 == 0, pltpu.roll(full, BLOCK, 1), full)
    high = base.astype(BF16).astype(F32)
    middle = (base - high).astype(BF16).astype(F32)
    low = (base - high - middle).astype(BF16).astype(F32)
    terms_ref[...] = jnp.where(rows8 < 2, high, jnp.where(rows8 < 4, middle, jnp.where(rows8 < 6, low, base)))


def share_kernel(terms_ref, parts_ref, out_ref):
    total = parts_ref[0].astype(F32)
    for source in range(1, parts_ref.shape[0]):
        total = total + parts_ref[source].astype(F32)
    part = terms_ref.shape[1]
    wide = total.shape[1]
    last = jnp.where(lanes(8, part) < BLOCK, total[:, wide - part :], terms_ref[...])
    send = jnp.concatenate([total[:, : wide - part], last], axis=1).astype(BF16)
    for target in range(out_ref.shape[0]):
        out_ref[target] = send


def held_at(block_row, row, n_rows):
    owner = block_row // n_rows
    distance = (owner // 2 - row // 2) & 7
    place = (jnp.int32(PLACES) >> (distance * 4)) & 7
    place = place + ((owner ^ row) & 1) * 8
    return place * n_rows + block_row % n_rows


def from_chip(distance, value):
    n_row = lax.axis_size("row")
    return lax.ppermute(value, "row", [(s, (s - 2 * distance) % n_row) for s in range(n_row)])


def pair_kernel(own_ref, other_ref, pair_ref):
    rows = own_ref.shape[0]
    pair_ref[0:rows, :] = own_ref[...]
    pair_ref[rows : 2 * rows, :] = other_ref[...]


def gather_strip(strip, across):
    n_row = lax.axis_size("row")
    rows, width = strip.shape
    pair = pl.pallas_call(
        pair_kernel,
        out_shape=jax.ShapeDtypeStruct((2 * rows, width), strip.dtype),
        in_specs=[VMEM, VMEM],
        out_specs=VMEM,
        compiler_params=pltpu.CompilerParams(vmem_limit_bytes=24 << 20),
        cost_estimate=pl.CostEstimate(flops=PAIR_COST, bytes_accessed=1 << 19, transcendentals=0),
        name="pair",
    )(strip, across)
    strip, pair = lax.optimization_barrier((strip, pair))
    above, below = from_chip(1, pair), from_chip(-1, pair)
    second, sixth = from_chip(2, strip), from_chip(-2, strip)
    held = jnp.concatenate([pair, second, sixth, above, below], axis=0)
    return held, lax.ppermute(held, "row", [(s, s ^ 1) for s in range(n_row)])


def plan_kernel(pat_ref, _, plan_ref):
    row, col, depth = (lax.axis_index(name) for name in ("row", "col", "depth"))
    n_rows, names = pat_ref.shape
    blocks = n_rows // lax.axis_size("depth")
    listed = pat_ref[...]
    own = row * n_rows + lax.broadcasted_iota(jnp.int32, (n_rows, 1), 0)
    bits = jnp.zeros((n_rows, 1), jnp.int32)
    for j in range(blocks):
        block = col * n_rows + depth * blocks + j
        hits = jnp.max(jnp.where(listed == block, 1, 0), axis=1, keepdims=True)
        bits = bits + jnp.where((hits == 1) | (own == block), 1 << j, 0)
    plan_ref[:, 0:names] = held_at(listed, row, n_rows) * BLOCK
    plan_ref[:, names : names + 1] = held_at(own, row, n_rows) * BLOCK
    plan_ref[:, names + 1 : names + 2] = bits


def product_kernel(
    plan_ref, flag_ref, count_ref, strip_ref, slots_ref, even_ref, odd_ref, out_ref, pop_ref, full
):
    n_rows, slots = plan_ref.shape[0], plan_ref.shape[1] - 1
    width = strip_ref.shape[1]
    which = lanes(BLOCK, width) // BLOCK
    half = even_ref.shape[0]
    full[0:half, :] = even_ref[...]
    full[half : 2 * half, :] = odd_ref[...]
    atoms = count_ref.shape[1]
    span = 2 * BLOCK
    wide = slots_ref.shape[1]
    low = lax.broadcasted_iota(jnp.int32, (atoms, atoms), 0)
    counts = jnp.broadcast_to(count_ref[...].astype(F32), (atoms, atoms))
    ends = jnp.sum(jnp.where(lanes(atoms, atoms) <= low, counts, 0.0), axis=1, keepdims=True)
    starts = jnp.sum(jnp.where(lanes(atoms, atoms) < low, counts, 0.0), axis=1, keepdims=True)
    at = lanes(atoms, span)
    total = jnp.zeros((atoms, span), F32)
    per_depth = 2 * BLOCK
    for d in range(n_rows // 2):
        terms = slots_ref[d * per_depth : (d + 1) * per_depth, wide - span :].astype(F32)
        terms = jnp.sum(terms.reshape(per_depth // 8, 8, span), axis=0)
        for u in range(2):
            squared = terms[u : u + 1] + terms[u + 2 : u + 3] + terms[u + 4 : u + 5]
            flag = jnp.broadcast_to(flag_ref[2 * d + u], squared.shape)
            diag = jnp.where(flag == 1, squared, 2.0 * terms[u + 6 : u + 7] - squared)
            diag = diag.astype(BF16).astype(F32)
            place = (at + ((2 * d + u) * BLOCK - BLOCK)).astype(F32)
            inside = (place >= starts) & (place < ends) & (at >= BLOCK)
            total = total + jnp.where(inside, jnp.broadcast_to(diag, (atoms, span)), 0.0)
    ones = jnp.ones((8, span), F32)
    sums = lax.dot_general(
        ones, total, (((1,), (1,)), ((), ())), precision=lax.Precision.HIGHEST, preferred_element_type=F32
    )
    pop_ref[...] = sums[0:1]
    for i in range(n_rows):
        here = pl.ds(i * BLOCK, BLOCK)
        squared = jnp.zeros((BLOCK, width), F32)
        for first in range(0, slots, GROUP):
            last = min(first + GROUP, slots)
            starts = [pl.multiple_of(plan_ref[i, slot], BLOCK) for slot in range(first, last)]
            chosen = jnp.concatenate([full[pl.ds(start, BLOCK), :] for start in starts], axis=0)
            values = slots_ref[here, first * BLOCK : last * BLOCK]
            squared = squared + jnp.dot(values, chosen, preferred_element_type=F32)
        keep = (plan_ref[i, slots] >> which) & 1
        own = strip_ref[here, :].astype(F32)
        flag = jnp.broadcast_to(flag_ref[i], squared.shape)
        value = jnp.where(flag == 1, squared, 2.0 * own - squared)
        out_ref[here, :] = jnp.where(keep == 1, value, 0.0).astype(BF16)


def per_device(density, pattern, orbital_counts, branch_flag):
    tile = density.shape[0]
    n_row, n_col, n_depth = (lax.axis_size(name) for name in ("row", "col", "depth"))
    width = tile // n_depth
    n_rows, names = pattern.shape
    slots_wide = (names + 2) * BLOCK
    limit = pltpu.CompilerParams(vmem_limit_bytes=24 << 20)
    strip, rows, slots = pl.pallas_call(
        pack_kernel,
        out_shape=(
            jax.ShapeDtypeStruct((tile, width), BF16),
            jax.ShapeDtypeStruct((width, tile), BF16),
            jax.ShapeDtypeStruct((width, slots_wide), BF16),
        ),
        in_specs=[HBM, HBM],
        out_specs=(VMEM, VMEM, VMEM),
        scratch_shapes=[
            pltpu.SMEM(pattern.shape, jnp.int32),
            pltpu.VMEM(pattern.shape, jnp.int32),
            pltpu.VMEM(density.shape, BF16),
            pltpu.VMEM((tile // BLOCK + 1, width, 2 * BLOCK), F32),
            pltpu.SemaphoreType.DMA((3,)),
        ],
        compiler_params=pltpu.CompilerParams(vmem_limit_bytes=60 << 20),
        name="pack",
    )(pattern, density)
    swap = [(r * n_col + c, c * n_col + r) for r in range(n_row) for c in range(n_col)]
    trans = lax.ppermute(strip, ("row", "col"), swap)
    chunk = width // n_col
    parts = lax.all_to_all(slots.reshape(n_col, chunk, slots_wide), "col", 0, 0)
    across = from_chip(4, strip)
    terms = pl.pallas_call(
        diagonal_kernel,
        out_shape=jax.ShapeDtypeStruct((8, width), F32),
        in_specs=[VMEM, VMEM],
        out_specs=VMEM,
        compiler_params=limit,
        cost_estimate=pl.CostEstimate(flops=COST, bytes_accessed=1 << 20, transcendentals=0),
        name="diagonal",
    )(rows, trans)
    send = pl.pallas_call(
        share_kernel,
        out_shape=jax.ShapeDtypeStruct((n_depth * n_col, chunk, slots_wide), BF16),
        in_specs=[VMEM, VMEM],
        out_specs=VMEM,
        compiler_params=limit,
        name="share",
    )(terms, parts)
    held, other = gather_strip(strip, across)
    stripe = lax.all_to_all(send, ("depth", "col"), 0, 0).reshape(tile, slots_wide)
    plan = pl.pallas_call(
        plan_kernel,
        out_shape=jax.ShapeDtypeStruct((n_rows, names + 2), jnp.int32),
        in_specs=[VMEM, pl.BlockSpec(memory_space=pl.ANY)],
        out_specs=VMEM,
        compiler_params=limit,
        cost_estimate=pl.CostEstimate(flops=1 << 31, bytes_accessed=1 << 12, transcendentals=0),
        name="plan",
    )(pattern, across)
    updated, populations = pl.pallas_call(
        product_kernel,
        out_shape=(
            jax.ShapeDtypeStruct((tile, width), BF16),
            jax.ShapeDtypeStruct((1, orbital_counts.shape[1]), F32),
        ),
        in_specs=[SMEM, SMEM, VMEM, VMEM, VMEM, VMEM, VMEM],
        out_specs=(VMEM, VMEM),
        scratch_shapes=[pltpu.VMEM((n_row * tile, width), BF16)],
        compiler_params=limit,
        name="product",
    )(plan, branch_flag, orbital_counts, strip, stripe, held, other)
    return (updated, populations.reshape(-1))


def solution(mesh):
    in_specs = (P("row", "col"), P("row", None), P("row", None), P("row"))
    out_specs = (P("row", ("col", "depth")), P("row"))
    return jax.shard_map(
        per_device, mesh=mesh, in_specs=in_specs, out_specs=out_specs, check_vma=False
    )
```
